128 devices in a mesh: shard: 32 (over y, x, core), replica: 4 (over z).
Axes of the slice: x: 4, y: 4, z: 4, core: 2. Of those that a mesh axis runs over, the one named last changes fastest.
Arguments:
- tokens: bfloat16 [32768, 768], P(('shard', 'replica')), may hold values from -6 to 6
- cotangent: bfloat16 [32768, 768], P(('shard', 'replica')), may hold values from -6 to 6
- w_qkv: bfloat16 [768, 2304], P('shard'), may hold values from -0.21875 to 0.21875
- b_qkv: bfloat16 [2304], P('shard'), may hold values from -1.796875 to 1.796875
- w_out: bfloat16 [768, 768], P('shard'), may hold values from -0.875 to 0.875
- b_out: bfloat16 [768], P('shard'), may hold values from -1.796875 to 1.796875
- w_up: bfloat16 [768, 3072], P('shard'), may hold values from -0.21875 to 0.21875
- b_up: bfloat16 [3072], P('shard'), may hold values from -1.796875 to 1.796875
- w_down: bfloat16 [3072, 768], P('shard'), may hold values from -0.15625 to 0.15625
- b_down: bfloat16 [768], P('shard'), may hold values from -1.796875 to 1.796875
- ln1_gain: bfloat16 [768], P('shard'), may hold values from 0.5 to 1.5
- ln1_bias: bfloat16 [768], P('shard'), may hold values from -1.1953125 to 1.1953125
- ln2_gain: bfloat16 [768], P('shard'), may hold values from 0.5 to 1.5
- ln2_bias: bfloat16 [768], P('shard'), may hold values from -1.1953125 to 1.1953125
- seq_device: int32 [256], replicated, may hold values from 0 to 127, as said below
- seq_lengths: int32 [256], replicated, may hold values from 1 to 224, as said below
- seq_offsets: int32 [256], replicated, may hold values from 0 to 255, as said below
Outputs:
- mixed: bfloat16 [32768, 768], P(('shard', 'replica'))
- grad_tokens: bfloat16 [32768, 768], P(('shard', 'replica'))
- grad_w_qkv: float32 [768, 2304], P('shard')
- grad_b_qkv: float32 [2304], P('shard')
- grad_w_out: float32 [768, 768], P('shard')
- grad_b_out: float32 [768], P('shard')
- grad_w_up: float32 [768, 3072], P('shard')
- grad_b_up: float32 [3072], P('shard')
- grad_w_down: float32 [3072, 768], P('shard')
- grad_b_down: float32 [768], P('shard')
- grad_ln1_gain: float32 [768], P('shard')
- grad_ln1_bias: float32 [768], P('shard')
- grad_ln2_gain: float32 [768], P('shard')
- grad_ln2_bias: float32 [768], P('shard')
The draws below stay inside these ranges and needn't reach their ends.
Inputs may be any that keep to these rules, and one draw needn't show every extreme that they name: `seq_device`: every device holds exactly two sequences. `seq_lengths`: some sequence in every draw has exactly 256 - 256 // 8 tokens. `seq_offsets`: A device's two sequences lie in its 256 slots without intersection and hold at most 256 tokens together; in every draw some device's two hold exactly 256.
All inputs are finite; a program needn't handle non-finite values.
Results may differ from the reference program's by a relative error of at most 0.023.
Values may be sent and summed in bfloat16 or wider, within the bound.
A program may use at most 128 MiB of HBM per device.

```python
import jax
import jax.numpy as jnp
from jax import lax

D = 768
HEADS = 12
HD = 64
ROT = 16
FF = 3072
CAP = 256
TOKENS = 32768
NSEQ = 256
DEVICES = 128


def sequence_plan(key):
    order = jax.random.permutation(jax.random.fold_in(key, 11), NSEQ).astype(jnp.int32)
    first = jax.random.randint(jax.random.fold_in(key, 12), (DEVICES,), CAP // 8, CAP - CAP // 8 + 1, dtype=jnp.int32)
    full_device = jax.random.randint(jax.random.fold_in(key, 13), (), 0, DEVICES, dtype=jnp.int32)
    is_full = jnp.arange(DEVICES, dtype=jnp.int32) == full_device
    first = jnp.where(is_full, CAP - CAP // 8, first)
    second = jax.random.randint(jax.random.fold_in(key, 14), (DEVICES,), 1, CAP - first + 1, dtype=jnp.int32)
    second = jnp.where(is_full, CAP // 8, second)
    spare = CAP - first - second
    lead = jax.random.randint(jax.random.fold_in(key, 15), (DEVICES,), 0, spare + 1, dtype=jnp.int32)
    between = jax.random.randint(jax.random.fold_in(key, 16), (DEVICES,), 0, spare - lead + 1, dtype=jnp.int32)
    later = lead + first + between
    device = order // 2
    second_slot = order % 2 == 1
    lengths = jnp.where(second_slot, second[device], first[device]).astype(jnp.int32)
    offsets = jnp.where(second_slot, later[device], lead[device]).astype(jnp.int32)
    return (device.astype(jnp.int32), lengths, offsets)


def draw_seq_device(key, part):
    return sequence_plan(key)[0]


def draw_seq_lengths(key, part):
    return sequence_plan(key)[1]


def draw_seq_offsets(key, part):
    return sequence_plan(key)[2]


def shard_levels(rng, extent, cuts, low, largest):
    def one(dim, shards_of):
        steps = jax.random.uniform(jax.random.fold_in(jax.random.fold_in(rng, 6), dim), (shards_of,), jnp.float32, low / len(cuts), largest / len(cuts))
        return jnp.repeat(jnp.exp(steps), extent[dim] // shards_of).reshape((-1,) + (1,) * (len(extent) - dim - 1))

    level = one(*cuts[0])
    for cut in cuts[1:]:
        level = level * one(*cut)
    return level


def scatter_about(own_key, extent, deviation, bound, split=(), kind=jnp.bfloat16):
    array = jax.random.normal(own_key, extent, jnp.float32) * deviation
    if len(split) > 0:
        array = shard_levels(own_key, extent, split, -0.22, 0.18) * array
    return jnp.clip(array, min=-bound, max=bound).astype(kind)


def setup_inputs(seed: int = 0) -> dict:
    arg_keys = jax.random.split(jax.random.key(seed), 18)
    tokens = scatter_about(arg_keys[0], (TOKENS, D), 1.0, 6.0, ((0, 128),))
    cotangent = scatter_about(arg_keys[1], (TOKENS, D), 1.0, 6.0, ((0, 128),))
    w_qkv = scatter_about(arg_keys[2], (D, 3 * D), D ** -0.5, 0.21875, ((0, 32),))
    b_qkv = scatter_about(arg_keys[3], (3 * D,), 0.3, 1.796875, ((0, 32),))
    w_out = scatter_about(arg_keys[4], (D, D), (D // 16) ** -0.5, 0.875, ((0, 32),))
    b_out = scatter_about(arg_keys[5], (D,), 0.3, 1.796875, ((0, 32),))
    w_up = scatter_about(arg_keys[6], (D, FF), D ** -0.5, 0.21875, ((0, 32),))
    b_up = scatter_about(arg_keys[7], (FF,), 0.3, 1.796875, ((0, 32),))
    w_down = scatter_about(arg_keys[8], (FF, D), (FF // 2) ** -0.5, 0.15625, ((0, 32),))
    b_down = scatter_about(arg_keys[9], (D,), 0.3, 1.796875, ((0, 32),))
    ln1_gain = jnp.clip(1.0 + 0.1 * jax.random.normal(arg_keys[10], (D,), jnp.float32), 0.5, 1.5).astype(jnp.bfloat16)
    ln1_bias = scatter_about(arg_keys[11], (D,), 0.2, 1.1953125, ((0, 32),))
    ln2_gain = jnp.clip(1.0 + 0.1 * jax.random.normal(arg_keys[12], (D,), jnp.float32), 0.5, 1.5).astype(jnp.bfloat16)
    ln2_bias = scatter_about(arg_keys[13], (D,), 0.2, 1.1953125, ((0, 32),))
    seq_device = draw_seq_device(jax.random.fold_in(arg_keys[17], 71), 0)
    seq_lengths = draw_seq_lengths(jax.random.fold_in(arg_keys[17], 71), 0)
    seq_offsets = draw_seq_offsets(jax.random.fold_in(arg_keys[17], 71), 0)
    return dict(tokens=tokens, cotangent=cotangent, w_qkv=w_qkv, b_qkv=b_qkv, w_out=w_out, b_out=b_out, w_up=w_up, b_up=b_up, w_down=w_down, b_down=b_down, ln1_gain=ln1_gain, ln1_bias=ln1_bias, ln2_gain=ln2_gain, ln2_bias=ln2_bias, seq_device=seq_device, seq_lengths=seq_lengths, seq_offsets=seq_offsets)


@jax.custom_vjp
def low(v):
    return lax.optimization_barrier(v.astype(jnp.bfloat16)).astype(jnp.float32)

@jax.custom_vjp
def low_back(v):
    return v

def low_keep(v):
    return (low(v), None)

def low_pass(kept, grad):
    return (grad,)

def back_keep(v):
    return (v, None)

def back_low(kept, grad):
    return (low(grad),)
low.defvjp(low_keep, low_pass)
low_back.defvjp(back_keep, back_low)
HIGH = lax.Precision.HIGHEST
EPS = 1e-05

def layer_norm(x, gain, bias):
    mean = lax.optimization_barrier(jnp.mean(x, axis=-1, keepdims=True))
    centered = x - mean
    var = lax.optimization_barrier(jnp.mean(centered * centered, axis=-1, keepdims=True))
    return centered * lax.rsqrt(var + EPS) * gain + bias

def rotate(value, cosine, sine):
    half = ROT // 2
    head = value[..., :ROT]
    turned = jnp.concatenate([-head[..., half:], head[..., :half]], axis=-1)
    return jnp.concatenate([head * cosine + turned * sine, value[..., ROT:]], axis=-1)

def token_tables(seq_device, seq_lengths, seq_offsets):
    slots = jnp.arange(CAP, dtype=jnp.int32)
    numbers = jnp.arange(NSEQ, dtype=jnp.int32)

    def one_device(device):
        inside = (seq_device == device)[:, None] & (slots[None, :] >= seq_offsets[:, None]) & (slots[None, :] < (seq_offsets + seq_lengths)[:, None])
        segment = lax.optimization_barrier(jnp.sum(jnp.where(inside, numbers[:, None] + 1, 0), axis=0)).astype(jnp.int32) - 1
        position = lax.optimization_barrier(jnp.sum(jnp.where(inside, slots[None, :] - seq_offsets[:, None], 0), axis=0)).astype(jnp.int32)
        return (segment, position)
    return lax.map(one_device, jnp.arange(DEVICES, dtype=jnp.int32))

def block(params, x, segment, position):
    w_qkv, b_qkv, w_out, b_out, w_up, b_up, w_down, b_down, g1, c1, g2, c2 = params
    half = ROT // 2
    xn1 = low(layer_norm(x, g1, c1))
    qkv = low_back(jnp.dot(xn1, w_qkv, precision=HIGH) + b_qkv)
    query = qkv[:, :D].reshape(CAP, HEADS, HD)
    key = qkv[:, D:2 * D].reshape(CAP, HEADS, HD)
    value = qkv[:, 2 * D:].reshape(CAP, HEADS, HD)
    freqs = 10000.0 ** (-(jnp.arange(half, dtype=jnp.float32) * 2.0) / ROT)
    angle = position.astype(jnp.float32)[:, None] * freqs[None, :]
    angle = jnp.concatenate([angle, angle], axis=-1)[:, None, :]
    cosine, sine = (jnp.cos(angle), jnp.sin(angle))
    query = low(rotate(query, cosine, sine))
    key = low(rotate(key, cosine, sine))
    value = low(value)
    scores = low_back(jnp.einsum('qhd,khd->hqk', query, key, precision=HIGH) * HD ** (-0.5))
    slots = jnp.arange(CAP, dtype=jnp.int32)
    allowed = (segment[:, None] == segment[None, :]) & (slots[None, :] <= slots[:, None])
    scores = jnp.where(allowed[None], scores, -1e+30)
    top = lax.optimization_barrier(jnp.max(scores, axis=-1, keepdims=True))
    lse = top + jnp.log(lax.optimization_barrier(jnp.sum(jnp.exp(scores - top), axis=-1, keepdims=True)))
    probs = low(jnp.exp(scores - lse))
    context = jnp.einsum('hqk,khd->qhd', probs, value, precision=HIGH).reshape(CAP, D)
    context = low(low_back(context))
    attn = jnp.dot(context, w_out, precision=HIGH) + b_out
    xn2 = low(layer_norm(x, g2, c2))
    hidden = low_back(jnp.dot(xn2, w_up, precision=HIGH) + b_up)
    act = low(jax.nn.gelu(hidden, approximate=False))
    mlp = jnp.dot(act, w_down, precision=HIGH) + b_down
    valid = (segment >= 0).astype(x.dtype)
    return valid[:, None] * (x + attn + mlp)

def reference(tokens, cotangent, w_qkv, b_qkv, w_out, b_out, w_up, b_up, w_down, b_down, ln1_gain, ln1_bias, ln2_gain, ln2_bias, seq_device, seq_lengths, seq_offsets):
    segment, position = token_tables(seq_device, seq_lengths, seq_offsets)
    params = tuple((w.astype(jnp.float32) for w in (w_qkv, b_qkv, w_out, b_out, w_up, b_up, w_down, b_down, ln1_gain, ln1_bias, ln2_gain, ln2_bias)))
    inputs = tokens.astype(jnp.float32).reshape(DEVICES, CAP, D)

    def forward(weights, rows):
        step = jax.checkpoint(block)

        def one(items):
            return step(weights, items[0], items[1], items[2])
        return lax.map(one, (rows, segment, position))
    result, pull = jax.vjp(forward, params, inputs)
    grads, grad_rows = pull(cotangent.astype(jnp.float32).reshape(DEVICES, CAP, D))
    mixed = result.reshape(DEVICES * CAP, D).astype(jnp.bfloat16)
    grad_tokens = grad_rows.reshape(DEVICES * CAP, D).astype(jnp.bfloat16)
    return (mixed, grad_tokens, grads[0], grads[1], grads[2], grads[3], grads[4], grads[5], grads[6], grads[7], grads[8], grads[9], grads[10], grads[11])
```

```python
import jax
import jax.numpy as jnp
from jax import lax
from jax.experimental import pallas as pl
from jax.experimental.pallas import tpu as pltpu
from jax.sharding import PartitionSpec as P

HD = 64
ROT = 16


EPS = 1e-05
INV_ROOT_TWO = 0.7071067811865476
INV_ROOT_TWO_PI = 0.3989422804014327


def norm_rows(x, gain, bias):
    mean = jnp.mean(x, axis=-1, keepdims=True)
    centered = x - mean
    var = jnp.mean(centered * centered, axis=-1, keepdims=True)
    inverse = lax.rsqrt(var + EPS)
    normal = centered * inverse
    return (normal * gain + bias, normal, inverse)


def norm_back(upstream, normal, inverse, gain):
    scaled = upstream * gain
    centre = jnp.mean(scaled, axis=-1, keepdims=True)
    slope = jnp.mean(scaled * normal, axis=-1, keepdims=True)
    return (
        inverse * (scaled - centre - normal * slope),
        jnp.sum(upstream * normal, axis=0),
        jnp.sum(upstream, axis=0),
    )


def rotate(value, cosine, sine):
    half = ROT // 2
    head = value[..., :ROT]
    turned = jnp.concatenate([-head[..., half:], head[..., :half]], axis=-1)
    return jnp.concatenate([head * cosine + turned * sine, value[..., ROT:]], axis=-1)


def unrotate(grad, cosine, sine):
    half = ROT // 2
    head = grad[..., :ROT]
    moved = head * sine
    back = jnp.concatenate([moved[..., half:], -moved[..., :half]], axis=-1)
    return jnp.concatenate([head * cosine + back, grad[..., ROT:]], axis=-1)


def token_tables(seq_device, seq_lengths, seq_offsets, device, rows):
    slots = jnp.arange(rows, dtype=jnp.int32)
    numbers = jnp.arange(seq_device.shape[0], dtype=jnp.int32)
    inside = (
        (seq_device == device)[:, None]
        & (slots[None, :] >= seq_offsets[:, None])
        & (slots[None, :] < (seq_offsets + seq_lengths)[:, None])
    )
    segment = jnp.sum(jnp.where(inside, numbers[:, None] + 1, 0), axis=0) - 1
    position = jnp.sum(jnp.where(inside, slots[None, :] - seq_offsets[:, None], 0), axis=0)
    return (segment, position)


def attention_scores(query, key, allowed):
    scores = jnp.einsum("qhd,khd->hqk", query, key, preferred_element_type=jnp.float32) * HD ** (
        -0.5
    )
    return jnp.where(allowed[None], scores, -1e30)


MESH = pl.DeviceIdType.MESH

UNIT = (48, 48, 48, 192, 16)
WIDTH = (2304, 768, 3072, 768, 768)
CUT = (640, 256, 768, 128, 256)
PARTS = 5


def place():
    index = lax.axis_index("shard")
    core = lax.rem(index, 2)
    chip = index // 2
    x = lax.rem(chip, 4)
    y = chip // 4
    first = x * (1 - core) + y * core
    second = y * (1 - core) + x * core
    return core, first, second, 1 + 3 * core, 4 - 3 * core


def around(value, shift):
    return lax.rem(value + shift + 4, 4)


def remote(source, target, sent, received, device):
    return pltpu.make_async_remote_copy(
        src_ref=source, dst_ref=target, send_sem=sent, recv_sem=received, device_id=device, device_id_type=MESH
    )


def gather_kernel(*refs):
    own = refs[:PARTS]
    full = refs[PARTS : 2 * PARTS]
    pair = refs[2 * PARTS : 3 * PARTS]
    unit = refs[3 * PARTS : 4 * PARTS]
    pair_send, pair_recv, send, recv, near_send, near_recv, keep = refs[4 * PARTS :]
    core, first, second, stride_a, stride_b = place()

    def chip(da, db):
        return around(first, da) * stride_a + around(second, db) * stride_b

    def device(da, db):
        return {"shard": chip(da, db) * 2 + core}

    sibling = {"shard": chip(0, 0) * 2 + 1 - core}

    def block(i, da, db, low=0, high=None):
        u, half = UNIT[i], WIDTH[i] // 2
        high = half if high is None else high
        return full[i].at[
            pl.ds(pl.multiple_of(chip(da, db) * u, 16), u),
            pl.ds(pl.multiple_of(core * half + low, 128), high - low),
        ]

    barrier = pltpu.get_barrier_semaphore()
    for target in (device(1, 0), device(-1, 0), device(0, 1), device(0, -1), sibling):
        pl.semaphore_signal(barrier, inc=1, device_id=target, device_id_type=MESH)
    pl.semaphore_wait(barrier, 5)

    started = []
    pairs = []
    for i in range(PARTS):
        half = WIDTH[i] // 2
        copy = remote(
            own[i].at[:, pl.ds(pl.multiple_of((1 - core) * half, 128), half)],
            pair[i],
            pair_send.at[i],
            pair_recv.at[i],
            sibling,
        )
        copy.start()
        pairs.append(copy)

    def push(i, slot, source, target, device_id, arrival):
        copy = remote(source, target, send.at[i, slot], recv.at[i, arrival], device_id)
        copy.start()
        started.append(copy)

    def arrived(i, slot, ref):
        remote(ref, ref, send.at[i, 0], recv.at[i, slot], sibling).wait_recv()

    def hand_over(i, da, db, source=None):
        target = block(i, da, db)
        remote(target if source is None else source, target, near_send.at[i], near_recv.at[i], sibling).start()

    keeps = []
    for i in range(PARTS):
        half = WIDTH[i] // 2
        pairs[i].wait_recv()
        mine = jnp.where(core == 0, own[i][:, :half], own[i][:, half:])
        other = pair[i][...]
        if i == 4:
            unit[i][...] = (mine + other).astype(jnp.bfloat16)
        else:
            rows = jnp.concatenate([jnp.where(core == 0, mine, other), jnp.where(core == 0, other, mine)], axis=0)
            unit[i][...] = rows.astype(jnp.bfloat16)
        here = block(i, 0, 0)
        push(i, 0, unit[i], here, device(1, 0), 0)
        push(i, 1, unit[i], here, device(-1, 0), 1)
        push(i, 2, unit[i], here, device(0, 1), 4)
        push(i, 3, unit[i], here, device(0, -1), 8)
        hand_over(i, 0, 0, unit[i])
        copy = pltpu.make_async_copy(unit[i], here, keep.at[i])
        copy.start()
        keeps.append(copy)
    for i in range(PARTS):
        half, cut = WIDTH[i] // 2, CUT[i]
        arrived(i, 0, block(i, -1, 0))
        push(i, 4, block(i, -1, 0, 0, cut), block(i, -1, 0, 0, cut), device(1, 0), 2)
        push(i, 5, block(i, -1, 0), block(i, -1, 0), device(0, 1), 5)
        push(i, 6, block(i, -1, 0), block(i, -1, 0), device(0, -1), 9)
        hand_over(i, -1, 0)
        arrived(i, 1, block(i, 1, 0))
        push(i, 7, block(i, 1, 0, cut, half), block(i, 1, 0, cut, half), device(-1, 0), 3)
        push(i, 8, block(i, 1, 0), block(i, 1, 0), device(0, 1), 6)
        push(i, 9, block(i, 1, 0), block(i, 1, 0), device(0, -1), 10)
        hand_over(i, 1, 0)
    for i in range(PARTS):
        half, cut = WIDTH[i] // 2, CUT[i]
        arrived(i, 4, block(i, 0, -1))
        push(i, 12, block(i, 0, -1), block(i, 0, -1), device(0, 1), 12)
        hand_over(i, 0, -1)
        arrived(i, 8, block(i, 0, 1))
        hand_over(i, 0, 1)
        arrived(i, 2, block(i, 2, 0, 0, cut))
        arrived(i, 3, block(i, 2, 0, cut, half))
        push(i, 10, block(i, 2, 0), block(i, 2, 0), device(0, 1), 7)
        push(i, 11, block(i, 2, 0), block(i, 2, 0), device(0, -1), 11)
        hand_over(i, 2, 0)
    for i in range(PARTS):
        arrived(i, 5, block(i, -1, -1))
        push(i, 13, block(i, -1, -1), block(i, -1, -1), device(0, 1), 13)
        hand_over(i, -1, -1)
        arrived(i, 9, block(i, -1, 1))
        hand_over(i, -1, 1)
        arrived(i, 10, block(i, 1, 1))
        push(i, 14, block(i, 1, 1), block(i, 1, 1), device(0, -1), 14)
        hand_over(i, 1, 1)
        arrived(i, 6, block(i, 1, -1))
        hand_over(i, 1, -1)
    for i in range(PARTS):
        arrived(i, 11, block(i, 2, 1))
        push(i, 15, block(i, 2, 1), block(i, 2, 1), device(0, -1), 15)
        hand_over(i, 2, 1)
        arrived(i, 7, block(i, 2, -1))
        hand_over(i, 2, -1)
        arrived(i, 12, block(i, 0, 2))
        hand_over(i, 0, 2)
    for i in range(PARTS):
        for slot, da in ((13, -1), (14, 1), (15, 2)):
            arrived(i, slot, block(i, da, 2))
            hand_over(i, da, 2)
    for i in range(PARTS):
        half = WIDTH[i] // 2
        mine = full[i].at[:, pl.ds(pl.multiple_of(core * half, 128), half)]
        other = full[i].at[:, pl.ds(pl.multiple_of((1 - core) * half, 128), half)]
        remote(mine, other, near_send.at[i], near_recv.at[i], sibling).wait()
        keeps[i].wait()
        pairs[i].wait_send()
    for copy in started:
        copy.wait_send()


def gather(w_qkv, w_out, w_up, w_down, small):
    own = [value.astype(jnp.float32) for value in (w_qkv, w_out, w_up, w_down, small)]
    vmem = pl.BlockSpec(memory_space=pltpu.VMEM)
    anywhere = pl.BlockSpec(memory_space=pl.ANY)
    return pl.pallas_call(
        gather_kernel,
        out_shape=[jax.ShapeDtypeStruct((16 * UNIT[i], WIDTH[i]), jnp.bfloat16) for i in range(PARTS)],
        in_specs=[vmem] * PARTS,
        out_specs=[anywhere] * PARTS,
        scratch_shapes=[pltpu.VMEM((own[i].shape[0], WIDTH[i] // 2), jnp.float32) for i in range(PARTS)]
        + [pltpu.VMEM((UNIT[i], WIDTH[i] // 2), jnp.bfloat16) for i in range(PARTS)]
        + [
            pltpu.SemaphoreType.DMA((PARTS,)),
            pltpu.SemaphoreType.DMA((PARTS,)),
            pltpu.SemaphoreType.DMA((PARTS, 16)),
            pltpu.SemaphoreType.DMA((PARTS, 16)),
            pltpu.SemaphoreType.DMA((PARTS,)),
            pltpu.SemaphoreType.DMA((PARTS,)),
            pltpu.SemaphoreType.DMA((PARTS,)),
        ],
        compiler_params=pltpu.CompilerParams(
            collective_id=0, has_side_effects=True, vmem_limit_bytes=24 * 1024 * 1024
        ),
    )(*own)


GRADS = 4
TILES = 36


def scatter_kernel(*refs):
    full = refs[:GRADS]
    small_ref = refs[GRADS]
    outs = refs[GRADS + 1 : 2 * GRADS + 1]
    small_out = refs[2 * GRADS + 1]
    rest = refs[2 * GRADS + 2 :]
    total = rest[:GRADS]
    pair = rest[GRADS : 2 * GRADS]
    far_b = rest[2 * GRADS : 3 * GRADS]
    near_b = rest[3 * GRADS : 4 * GRADS]
    far_a = rest[4 * GRADS : 5 * GRADS]
    near_a = rest[5 * GRADS : 6 * GRADS]
    last = rest[6 * GRADS : 7 * GRADS]
    (
        part, parts_in, whole, small_in, small_sum,
        local, pair_send, pair_recv, send, recv, z_send, z_recv, small_send, small_recv, out_send, out_recv, out_local,
    ) = rest[7 * GRADS :]
    core, first, second, stride_a, stride_b = place()
    depth = lax.axis_index("replica")

    def chip(da, db):
        return around(first, da) * stride_a + around(second, db) * stride_b

    def device(da, db):
        return {"shard": chip(da, db) * 2 + core}

    def deep(dz):
        return {"replica": around(depth, dz)}

    sibling = {"shard": chip(0, 0) * 2 + 1 - core}

    def half_of(i, which):
        half = WIDTH[i] // 2
        return full[i].at[:, pl.ds(pl.multiple_of(which * half, 128), half)]

    def rows(i, where):
        return pl.ds(pl.multiple_of(where * UNIT[i], 16), UNIT[i])

    def in_line(i, a, db):
        return rows(i, a * stride_a + around(second, db) * stride_b)

    barrier = pltpu.get_barrier_semaphore()
    targets = [device(1, 0), device(-1, 0), device(2, 0), device(0, 1), device(0, -1), device(0, 2), sibling]
    targets += [deep(1), deep(2), deep(3)]
    for target in targets:
        pl.semaphore_signal(barrier, inc=1, device_id=target, device_id_type=MESH)
    pl.semaphore_wait(barrier, len(targets))

    started = []

    def start(source, target, sent, received, device_id):
        copy = remote(source, target, sent, received, device_id)
        copy.start()
        started.append(copy)

    def arrived(ref, received):
        remote(ref, ref, send.at[0, 0], received, sibling).wait_recv()

    loads = []
    for i in range(GRADS):
        start(half_of(i, 1 - core), pair[i], pair_send.at[i], pair_recv.at[i], sibling)
        copy = pltpu.make_async_copy(half_of(i, core), total[i], local.at[i])
        copy.start()
        loads.append(copy)
    start(small_ref, small_in.at[0], small_send.at[0], small_recv.at[0], sibling)

    def small_step(step, count, others):
        base = 0 if step == 0 else 3 * step - 2
        for n in range(count):
            arrived(small_in.at[base + n], small_recv.at[base + n])
        value = small_ref[...] if step == 0 else small_sum[step - 1]
        for n in range(count):
            value = value + small_in[base + n]
        small_sum[step] = value
        if others is not None:
            base = 3 * step + 1
            for n, target in enumerate(others):
                start(small_sum.at[step], small_in.at[base + n], small_send.at[base + n], small_recv.at[base + n], target)

    def add_rows(i, where, extra):
        total[i][where, :] = (total[i][where, :].astype(jnp.float32) + extra.astype(jnp.float32)).astype(jnp.bfloat16)

    def add_pair(i, db):
        for a in range(4):
            where = in_line(i, a, db)
            add_rows(i, where, pair[i][where, :])

    for i in range(GRADS):
        loads[i].wait()
        arrived(pair[i], pair_recv.at[i])
        add_pair(i, 2)
        for n, a in enumerate((0, 1)):
            start(total[i].at[in_line(i, a, 2), :], far_b[i].at[n], send.at[i, n], recv.at[i, n], device(0, 1))
        for n, a in enumerate((2, 3)):
            start(total[i].at[in_line(i, a, 2), :], far_b[i].at[2 + n], send.at[i, 2 + n], recv.at[i, 2 + n], device(0, -1))
        add_pair(i, 1)
        for a in (2, 3):
            start(total[i].at[in_line(i, a, 1), :], near_b[i].at[a], send.at[i, 4 + a], recv.at[i, 4 + a], device(0, 1))
        add_pair(i, -1)
        for a in (0, 1):
            start(total[i].at[in_line(i, a, -1), :], near_b[i].at[4 + a], send.at[i, 8 + a], recv.at[i, 8 + a], device(0, -1))
        if i == 0:
            small_step(0, 1, (device(1, 0), device(2, 0), device(-1, 0)))
    for i in range(GRADS):
        for n, a in enumerate((0, 1)):
            arrived(far_b[i].at[n], recv.at[i, n])
            add_rows(i, in_line(i, a, 1), far_b[i][n])
            start(total[i].at[in_line(i, a, 1), :], near_b[i].at[a], send.at[i, 4 + a], recv.at[i, 4 + a], device(0, 1))
        for n, a in enumerate((2, 3)):
            arrived(far_b[i].at[2 + n], recv.at[i, 2 + n])
            add_rows(i, in_line(i, a, -1), far_b[i][2 + n])
            start(total[i].at[in_line(i, a, -1), :], near_b[i].at[4 + a], send.at[i, 8 + a], recv.at[i, 8 + a], device(0, -1))
        add_pair(i, 0)
    small_step(1, 3, (device(0, 1), device(0, 2), device(0, -1)))
    for i in range(GRADS):
        half, cut = WIDTH[i] // 2, CUT[i]
        for n in range(8):
            arrived(near_b[i].at[n], recv.at[i, 4 + n])

        def here(da, db=0):
            return rows(i, chip(da, db))

        for a in range(4):
            where = in_line(i, a, 0)
            value = total[i][where, :].astype(jnp.float32) + near_b[i][a].astype(jnp.float32)
            total[i][where, :] = (value + near_b[i][4 + a].astype(jnp.float32)).astype(jnp.bfloat16)
        start(total[i].at[here(2), pl.ds(0, cut)], far_a[i].at[:, pl.ds(0, cut)], send.at[i, 12], recv.at[i, 12], device(1, 0))
        start(
            total[i].at[here(2), pl.ds(cut, half - cut)],
            far_a[i].at[:, pl.ds(cut, half - cut)],
            send.at[i, 13],
            recv.at[i, 13],
            device(-1, 0),
        )
    small_step(2, 3, (deep(1), deep(2), deep(3)))
    for i in range(GRADS):
        half, cut = WIDTH[i] // 2, CUT[i]
        low, high = pl.ds(0, cut), pl.ds(cut, half - cut)
        one, other = rows(i, chip(1, 0)), rows(i, chip(-1, 0))
        arrived(far_a[i].at[:, low], recv.at[i, 12])
        value = total[i][one, low].astype(jnp.float32) + far_a[i][:, low].astype(jnp.float32)
        total[i][one, low] = value.astype(jnp.bfloat16)
        start(total[i].at[one, :], near_a[i].at[0], send.at[i, 14], recv.at[i, 14], device(1, 0))
        arrived(far_a[i].at[:, high], recv.at[i, 13])
        value = total[i][other, high].astype(jnp.float32) + far_a[i][:, high].astype(jnp.float32)
        total[i][other, high] = value.astype(jnp.bfloat16)
        start(total[i].at[other, :], near_a[i].at[1], send.at[i, 15], recv.at[i, 15], device(-1, 0))

    def tiles():
        n = 0
        for i in range(GRADS):
            for r in range(UNIT[i] // 48):
                for t in range(WIDTH[i] // 256):
                    yield n, i, slice(48 * r, 48 * r + 48), slice(128 * t, 128 * t + 128)
                    n += 1

    for i in range(GRADS):
        arrived(near_a[i].at[0], recv.at[i, 14])
        arrived(near_a[i].at[1], recv.at[i, 15])
        mine = total[i][rows(i, chip(0, 0)), :].astype(jnp.float32)
        last[i][...] = mine + near_a[i][0].astype(jnp.float32) + near_a[i][1].astype(jnp.float32)
    for n, i, r, c in tiles():
        part[n] = last[i][r, c].astype(jnp.bfloat16)
    quarter = TILES // 4

    def share(dz):
        return pl.ds(around(depth, dz) * quarter, quarter)

    for n in range(3):
        start(part.at[share(n + 1)], parts_in.at[n], z_send.at[n], z_recv.at[n], deep(n + 1))
    small_step(3, 3, None)
    small_out[...] = small_sum[3]
    value = part[share(0)].astype(jnp.float32)
    for n in range(3):
        arrived(parts_in.at[n], z_recv.at[n])
        value = value + parts_in[n].astype(jnp.float32)
    whole[share(0)] = value.astype(jnp.bfloat16)
    for n in range(3):
        start(whole.at[share(0)], whole.at[share(0)], z_send.at[3 + n], z_recv.at[3 + n], deep(n + 1))
    for n in range(3):
        arrived(whole.at[share(-n - 1)], z_recv.at[3 + n])
    for n, i, r, c in tiles():
        last[i][r, c] = whole[n].astype(jnp.float32)
    finals = []
    for i in range(GRADS):
        half, own = WIDTH[i] // 2, UNIT[i] // 2
        columns = pl.ds(pl.multiple_of(core * half, 128), half)
        copy = remote(
            last[i].at[pl.ds(pl.multiple_of((1 - core) * own, 8), own), :],
            outs[i].at[:, columns],
            out_send.at[i],
            out_recv.at[i],
            sibling,
        )
        copy.start()
        finals.append(copy)
        copy = pltpu.make_async_copy(
            last[i].at[pl.ds(pl.multiple_of(core * own, 8), own), :], outs[i].at[:, columns], out_local.at[i]
        )
        copy.start()
        finals.append(copy)
    for copy in finals:
        copy.wait()
    for copy in started:
        copy.wait_send()


def scatter(grads, small):
    vmem = pl.BlockSpec(memory_space=pltpu.VMEM)
    anywhere = pl.BlockSpec(memory_space=pl.ANY)
    index = range(GRADS)
    half = [WIDTH[i] // 2 for i in index]
    low = jnp.bfloat16
    dma = pltpu.SemaphoreType.DMA
    return pl.pallas_call(
        scatter_kernel,
        out_shape=[jax.ShapeDtypeStruct((UNIT[i] // 2, WIDTH[i]), jnp.float32) for i in index]
        + [jax.ShapeDtypeStruct(small.shape, jnp.float32)],
        in_specs=[anywhere] * GRADS + [vmem],
        out_specs=[anywhere] * GRADS + [vmem],
        scratch_shapes=[pltpu.VMEM((16 * UNIT[i], half[i]), low) for i in index]
        + [pltpu.VMEM((16 * UNIT[i], half[i]), low) for i in index]
        + [pltpu.VMEM((4, UNIT[i], half[i]), low) for i in index]
        + [pltpu.VMEM((8, UNIT[i], half[i]), low) for i in index]
        + [pltpu.VMEM((UNIT[i], half[i]), low) for i in index]
        + [pltpu.VMEM((2, UNIT[i], half[i]), low) for i in index]
        + [pltpu.VMEM((UNIT[i], half[i]), jnp.float32) for i in index]
        + [
            pltpu.VMEM((TILES, 48, 128), low),
            pltpu.VMEM((3, TILES // 4, 48, 128), low),
            pltpu.VMEM((TILES, 48, 128), low),
            pltpu.VMEM((10, 16, 768), jnp.float32),
            pltpu.VMEM((4, 16, 768), jnp.float32),
            dma((GRADS,)),
            dma((GRADS,)),
            dma((GRADS,)),
            dma((GRADS, 16)),
            dma((GRADS, 16)),
            dma((6,)),
            dma((6,)),
            dma((10,)),
            dma((10,)),
            dma((GRADS,)),
            dma((GRADS,)),
            dma((GRADS,)),
        ],
        compiler_params=pltpu.CompilerParams(
            collective_id=1, has_side_effects=True, vmem_limit_bytes=48 * 1024 * 1024
        ),
    )(*grads, small)


def per_device(
    tokens,
    cotangent,
    w_qkv,
    b_qkv,
    w_out,
    b_out,
    w_up,
    b_up,
    w_down,
    b_down,
    ln1_gain,
    ln1_bias,
    ln2_gain,
    ln2_bias,
    seq_device,
    seq_lengths,
    seq_offsets,
):
    rows = tokens.shape[0]
    width = tokens.shape[1]
    heads = width // HD
    half = ROT // 2
    values = (b_qkv, b_up, b_out, b_down, ln1_gain, ln1_bias, ln2_gain, ln2_bias)
    index = lax.axis_index("shard")
    small = jnp.concatenate(
        [
            lax.dynamic_update_slice(
                jnp.zeros((value.shape[0] * 32,), jnp.float32), value.astype(jnp.float32), (index * value.shape[0],)
            )
            for value in values
        ]
        + [jnp.zeros((3 * width,), jnp.float32)]
    ).reshape(16, width)
    wq_all, wo_all, wu_all, wd_all, small_all = gather(w_qkv, w_out, w_up, w_down, small)
    small_all = jnp.sum(small_all.astype(jnp.float32).reshape(16, 16, width), axis=0)
    bq_all = small_all[0:3].reshape(3 * width)
    bu_all = small_all[3:7].reshape(4 * width)
    bo_all, bd_all, g1_all, c1_all, g2_all, c2_all = (small_all[row] for row in range(7, 13))
    device = lax.axis_index("shard") * lax.axis_size("replica") + lax.axis_index("replica")
    segment, position = token_tables(seq_device, seq_lengths, seq_offsets, device, rows)
    valid = (segment >= 0).astype(jnp.float32)
    slots = jnp.arange(rows, dtype=jnp.int32)
    allowed = (segment[:, None] == segment[None, :]) & (slots[None, :] <= slots[:, None])
    freqs = 10000.0 ** (-(jnp.arange(half, dtype=jnp.float32) * 2.0) / ROT)
    angle = position.astype(jnp.float32)[:, None] * freqs[None, :]
    angle = jnp.concatenate([angle, angle], axis=-1)[:, None, :]
    cosine, sine = (jnp.cos(angle), jnp.sin(angle))
    x = tokens.astype(jnp.float32)
    normed1, normal1, inverse1 = norm_rows(
        x, g1_all.astype(jnp.float32), c1_all.astype(jnp.float32)
    )
    normed2, normal2, inverse2 = norm_rows(
        x, g2_all.astype(jnp.float32), c2_all.astype(jnp.float32)
    )
    xn1 = normed1.astype(jnp.bfloat16)
    xn2 = normed2.astype(jnp.bfloat16)
    qkv = jnp.dot(xn1, wq_all, preferred_element_type=jnp.float32) + bq_all.astype(jnp.float32)
    query = rotate(qkv[:, :width].reshape(rows, heads, HD), cosine, sine).astype(jnp.bfloat16)
    key = rotate(qkv[:, width : 2 * width].reshape(rows, heads, HD), cosine, sine).astype(
        jnp.bfloat16
    )
    value = qkv[:, 2 * width :].reshape(rows, heads, HD).astype(jnp.bfloat16)
    scores = attention_scores(query, key, allowed)
    top = jnp.max(scores, axis=-1, keepdims=True)
    lse = top + jnp.log(jnp.sum(jnp.exp(scores - top), axis=-1, keepdims=True))
    probs = jnp.exp(scores - lse).astype(jnp.bfloat16)
    context = (
        jnp.einsum("hqk,khd->qhd", probs, value, preferred_element_type=jnp.float32)
        .reshape(rows, width)
        .astype(jnp.bfloat16)
    )
    attn = jnp.dot(context, wo_all, preferred_element_type=jnp.float32) + bo_all.astype(jnp.float32)
    hidden = jnp.dot(xn2, wu_all, preferred_element_type=jnp.float32) + bu_all.astype(jnp.float32)
    normal_cdf = 0.5 * (1.0 + lax.erf(hidden * INV_ROOT_TWO))
    act = (hidden * normal_cdf).astype(jnp.bfloat16)
    mlp = jnp.dot(act, wd_all, preferred_element_type=jnp.float32) + bd_all.astype(jnp.float32)
    mixed = (valid[:, None] * (x + attn + mlp)).astype(jnp.bfloat16)
    upstream = cotangent.astype(jnp.float32) * valid[:, None]
    upstream_low = upstream.astype(jnp.bfloat16)
    grad_bias_end = jnp.sum(upstream, axis=0)
    grad_w_out = jnp.einsum("ti,tj->ij", context, upstream_low, preferred_element_type=jnp.float32)
    grad_w_down = jnp.einsum("tf,tj->fj", act, upstream_low, preferred_element_type=jnp.float32)
    grad_act = jnp.einsum("tj,fj->tf", upstream_low, wd_all, preferred_element_type=jnp.float32)
    gelu_slope = normal_cdf + hidden * jnp.exp(-0.5 * hidden * hidden) * INV_ROOT_TWO_PI
    grad_hidden = (grad_act * gelu_slope).astype(jnp.bfloat16)
    grad_b_up = jnp.sum(grad_hidden.astype(jnp.float32), axis=0)
    grad_w_up = jnp.einsum("ti,tf->if", xn2, grad_hidden, preferred_element_type=jnp.float32)
    grad_xn2 = jnp.einsum("tf,if->ti", grad_hidden, wu_all, preferred_element_type=jnp.float32)
    grad_context = jnp.einsum(
        "tj,ij->ti", upstream_low, wo_all, preferred_element_type=jnp.float32
    )
    grad_context = grad_context.astype(jnp.bfloat16).reshape(rows, heads, HD)
    again_scores = attention_scores(query, key, allowed)
    weights_soft = jnp.exp(again_scores - lse)
    grad_value = jnp.einsum(
        "hqk,qhd->khd",
        weights_soft.astype(jnp.bfloat16),
        grad_context,
        preferred_element_type=jnp.float32,
    )
    grad_probs = jnp.einsum("qhd,khd->hqk", grad_context, value, preferred_element_type=jnp.float32)
    grad_scores = weights_soft * (
        grad_probs - jnp.sum(weights_soft * grad_probs, axis=-1, keepdims=True)
    )
    grad_scores = grad_scores.astype(jnp.bfloat16)
    grad_query = jnp.einsum(
        "hqk,khd->qhd", grad_scores, key, preferred_element_type=jnp.float32
    ) * HD ** (-0.5)
    grad_key = jnp.einsum(
        "hqk,qhd->khd", grad_scores, query, preferred_element_type=jnp.float32
    ) * HD ** (-0.5)
    grad_query = unrotate(grad_query, cosine, sine).reshape(rows, width)
    grad_key = unrotate(grad_key, cosine, sine).reshape(rows, width)
    grad_qkv = jnp.concatenate(
        [grad_query, grad_key, grad_value.reshape(rows, width)], axis=1
    ).astype(jnp.bfloat16)
    grad_b_qkv = jnp.sum(grad_qkv.astype(jnp.float32), axis=0)
    grad_w_qkv = jnp.einsum("ti,tc->ic", xn1, grad_qkv, preferred_element_type=jnp.float32)
    grad_xn1 = jnp.einsum("tc,ic->ti", grad_qkv, wq_all, preferred_element_type=jnp.float32)
    back_one, grad_g1, grad_c1 = norm_back(grad_xn1, normal1, inverse1, g1_all.astype(jnp.float32))
    back_two, grad_g2, grad_c2 = norm_back(grad_xn2, normal2, inverse2, g2_all.astype(jnp.float32))
    grad_tokens = (upstream + back_one + back_two).astype(jnp.bfloat16)
    small_grad = jnp.concatenate(
        [grad_b_qkv, grad_b_up, grad_bias_end, grad_g1, grad_c1, grad_g2, grad_c2, jnp.zeros((4 * width,), jnp.float32)]
    ).reshape(16, width)
    low = jnp.bfloat16
    out_qkv, out_out, out_up, out_down, small_out = scatter(
        [grad_w_qkv.astype(low), grad_w_out.astype(low), grad_w_up.astype(low), grad_w_down.astype(low)], small_grad
    )
    flat = small_out.reshape(16 * width)

    def owned(row, size):
        return lax.dynamic_slice(flat, (row * width + index * size,), (size,))

    end = owned(7, 24)
    return (
        mixed,
        grad_tokens,
        out_qkv,
        owned(0, 72),
        out_out,
        end,
        out_up,
        owned(3, 96),
        out_down,
        end,
        owned(8, 24),
        owned(9, 24),
        owned(10, 24),
        owned(11, 24),
    )


def solution(mesh):
    return jax.shard_map(
        per_device,
        mesh=mesh,
        in_specs=(
            P(("shard", "replica"), None),
            P(("shard", "replica"), None),
            P("shard", None),
            P("shard"),
            P("shard", None),
            P("shard"),
            P("shard", None),
            P("shard"),
            P("shard", None),
            P("shard"),
            P("shard"),
            P("shard"),
            P("shard"),
            P("shard"),
            P(),
            P(),
            P(),
        ),
        out_specs=(
            P(("shard", "replica"), None),
            P(("shard", "replica"), None),
            P("shard", None),
            P("shard"),
            P("shard", None),
            P("shard"),
            P("shard", None),
            P("shard"),
            P("shard", None),
            P("shard"),
            P("shard"),
            P("shard"),
            P("shard"),
            P("shard"),
        ),
        check_vma=False,
    )
```

```python
import types

import jax
import jax.numpy as jnp
from jax import lax
from jax.experimental import pallas as pl
from jax.experimental.pallas import tpu as pltpu
from jax.sharding import PartitionSpec as P

HD = 64
ROT = 16
WIDE = 768
ROWS = 256
EPS = 1e-05
INV_ROOT_TWO = 0.7071067811865476
INV_ROOT_TWO_PI = 0.3989422804014327
MESH = pl.DeviceIdType.MESH
F32 = jnp.float32
LOW = jnp.bfloat16

UNIT = (48, 48, 48, 192, 16)
WIDTH = (2304, 768, 3072, 768, 768)
CUT = (640, 256, 768, 128, 256)
QKV, OUT, UP, DOWN, SMALL = range(5)
PARTS = 5
GRADS = 4
GROUPS = ((OUT, QKV), (DOWN,), (UP,))
SHARE = 3


def mm(a, b):
    return jnp.dot(a, b, preferred_element_type=F32)


def mm_nt(a, b):
    return lax.dot_general(a, b, (((1,), (1,)), ((), ())), preferred_element_type=F32)


def mm_tn(a, b):
    return lax.dot_general(a, b, (((0,), (0,)), ((), ())), preferred_element_type=F32)


def around(value, shift):
    return lax.rem(value + shift + 4, 4)


def remote(source, target, sent, received, device):
    return pltpu.make_async_remote_copy(
        src_ref=source, dst_ref=target, send_sem=sent, recv_sem=received, device_id=device, device_id_type=MESH
    )


def scratch():
    dma = pltpu.SemaphoreType.DMA
    half = [width // 2 for width in WIDTH]
    own = [UNIT[i] // 2 for i in range(GRADS)] + [16]

    def each(count, shape, dtype=LOW):
        return [pltpu.VMEM(shape(i), dtype) for i in range(count)]

    groups = len(GROUPS)
    return dict(
        mine=each(PARTS, lambda i: (own[i], WIDTH[i]), F32),
        his=each(PARTS, lambda i: (own[i], half[i]), F32),
        unit=each(PARTS, lambda i: (UNIT[i], half[i])),
        full=each(PARTS, lambda i: (16 * UNIT[i], WIDTH[i])),
        total=each(GRADS, lambda i: (16 * UNIT[i], half[i])),
        away=each(GRADS, lambda i: (16 * UNIT[i], half[i])),
        pair=each(GRADS, lambda i: (16 * UNIT[i], half[i])),
        far_b=each(GRADS, lambda i: (4, UNIT[i], half[i])),
        near_b=each(GRADS, lambda i: (8, UNIT[i], half[i])),
        far_a=each(GRADS, lambda i: (UNIT[i], half[i])),
        near_a=each(GRADS, lambda i: (2, UNIT[i], half[i])),
        last=each(GRADS, lambda i: (UNIT[i], half[i]), F32),
        part=pltpu.VMEM((groups, 4 * SHARE, 48, 128), LOW),
        parts_in=pltpu.VMEM((groups, 3, SHARE, 48, 128), LOW),
        whole=pltpu.VMEM((groups, 4 * SHARE, 48, 128), LOW),
        small_grad=pltpu.VMEM((16, WIDE), F32),
        small_in=pltpu.VMEM((10, 16, WIDE), F32),
        small_sum=pltpu.VMEM((3, 16, WIDE), F32),
        vectors=pltpu.VMEM((16, WIDE), F32),
        normal=pltpu.VMEM((ROWS, WIDE), F32),
        inverse=pltpu.VMEM((ROWS, 1), F32),
        valid=pltpu.VMEM((ROWS, 1), F32),
        bias=pltpu.VMEM((ROWS, ROWS), F32),
        turn=pltpu.VMEM((3, ROWS, 128), F32),
        upstream=pltpu.VMEM((ROWS, WIDE), LOW),
        xn1=pltpu.VMEM((ROWS, WIDE), LOW),
        xn2=pltpu.VMEM((ROWS, WIDE), LOW),
        xt=pltpu.VMEM((WIDE, ROWS), LOW),
        qkv=pltpu.VMEM((ROWS, 3 * WIDE), LOW),
        dcontext=pltpu.VMEM((ROWS, WIDE), LOW),
        context=pltpu.VMEM((ROWS, WIDE), LOW),
        dqkv=pltpu.VMEM((ROWS, 3 * WIDE), LOW),
        act=pltpu.VMEM((ROWS, 4 * WIDE), LOW),
        slope=pltpu.VMEM((ROWS, 4 * WIDE), F32),
        dh=pltpu.VMEM((ROWS, 4 * WIDE), LOW),
        dx=pltpu.VMEM((ROWS, WIDE), F32),
        pair_send=dma((PARTS,)),
        pair_recv=dma((PARTS,)),
        send=dma((PARTS, 16)),
        recv=dma((PARTS, 16)),
        near_send=dma((PARTS,)),
        near_recv=dma((PARTS,)),
        keep=dma((PARTS,)),
        swap_send=dma((GRADS,)),
        swap_recv=dma((GRADS,)),
        back_send=dma((GRADS, 16)),
        back_recv=dma((GRADS, 16)),
        z_send=dma((groups, 6)),
        z_recv=dma((groups, 6)),
        small_send=dma((10,)),
        small_recv=dma((10,)),
        out_send=dma((GRADS,)),
        out_recv=dma((GRADS,)),
        out_local=dma((GRADS,)),
    )


KINDS, TREE = jax.tree.flatten(scratch())
SIZES = (72, 96, 24, 24, 24, 24, 24, 24)


def kernel(*refs):
    tokens, cotangent, packed, sequences = refs[:4]
    own = refs[4:8]
    mixed, grad_tokens = refs[8:10]
    outs = refs[10:14]
    small_out = refs[14]
    b = types.SimpleNamespace(**jax.tree.unflatten(TREE, refs[15:]))

    index = lax.axis_index("shard")
    depth = lax.axis_index("replica")
    core = lax.rem(index, 2)
    place = index // 2
    across, along = lax.rem(place, 4), place // 4
    first = across * (1 - core) + along * core
    second = along * (1 - core) + across * core
    stride_a, stride_b = 1 + 3 * core, 4 - 3 * core

    def chip(da, db):
        return around(first, da) * stride_a + around(second, db) * stride_b

    def device(da, db):
        return {"shard": chip(da, db) * 2 + core}

    def deep(dz):
        return {"replica": around(depth, dz)}

    sibling = {"shard": place * 2 + 1 - core}
    started = []

    def start(source, target, sent, received, device_id):
        copy = remote(source, target, sent, received, device_id)
        copy.start()
        started.append(copy)

    def arrived(ref, received):
        remote(ref, ref, b.send.at[0, 0], received, sibling).wait_recv()

    def columns(i, which):
        half = WIDTH[i] // 2
        return pl.ds(pl.multiple_of(which * half, 128), half)

    def block(i, da, db, low=0, high=None):
        u, half = UNIT[i], WIDTH[i] // 2
        high = half if high is None else high
        return b.full[i].at[
            pl.ds(pl.multiple_of(chip(da, db) * u, 16), u),
            pl.ds(pl.multiple_of(core * half + low, 128), high - low),
        ]

    def push(i, slot, source, target, device_id, arrival):
        start(source, target, b.send.at[i, slot], b.recv.at[i, arrival], device_id)

    def hand_over(i, da, db, source=None):
        target = block(i, da, db)
        source = target if source is None else source
        remote(source, target, b.near_send.at[i], b.near_recv.at[i], sibling).start()

    def take(i, slot, ref):
        arrived(ref, b.recv.at[i, slot])

    def swap_own(i):
        start(b.mine[i].at[:, columns(i, 1 - core)], b.his[i], b.pair_send.at[i], b.pair_recv.at[i], sibling)

    def g1(i):
        mine_ref, unit = b.mine[i], b.unit[i]
        arrived(b.his[i], b.pair_recv.at[i])
        half = WIDTH[i] // 2
        mine = jnp.where(core == 0, mine_ref[:, :half], mine_ref[:, half:])
        other = b.his[i][...]
        if i == SMALL:
            unit[...] = (mine + other).astype(LOW)
        else:
            rows = [jnp.where(core == 0, mine, other), jnp.where(core == 0, other, mine)]
            unit[...] = jnp.concatenate(rows, axis=0).astype(LOW)
        here = block(i, 0, 0)
        push(i, 0, unit, here, device(1, 0), 0)
        push(i, 1, unit, here, device(-1, 0), 1)
        push(i, 2, unit, here, device(0, 1), 4)
        push(i, 3, unit, here, device(0, -1), 8)
        hand_over(i, 0, 0, unit)
        pltpu.make_async_copy(unit, here, b.keep.at[i]).start()

    def g2(i):
        half, cut = WIDTH[i] // 2, CUT[i]
        take(i, 0, block(i, -1, 0))
        push(i, 4, block(i, -1, 0, 0, cut), block(i, -1, 0, 0, cut), device(1, 0), 2)
        push(i, 5, block(i, -1, 0), block(i, -1, 0), device(0, 1), 5)
        push(i, 6, block(i, -1, 0), block(i, -1, 0), device(0, -1), 9)
        hand_over(i, -1, 0)
        take(i, 1, block(i, 1, 0))
        push(i, 7, block(i, 1, 0, cut, half), block(i, 1, 0, cut, half), device(-1, 0), 3)
        push(i, 8, block(i, 1, 0), block(i, 1, 0), device(0, 1), 6)
        push(i, 9, block(i, 1, 0), block(i, 1, 0), device(0, -1), 10)
        hand_over(i, 1, 0)

    def g3(i):
        half, cut = WIDTH[i] // 2, CUT[i]
        take(i, 4, block(i, 0, -1))
        push(i, 12, block(i, 0, -1), block(i, 0, -1), device(0, 1), 12)
        hand_over(i, 0, -1)
        take(i, 8, block(i, 0, 1))
        hand_over(i, 0, 1)
        take(i, 2, block(i, 2, 0, 0, cut))
        take(i, 3, block(i, 2, 0, cut, half))
        push(i, 10, block(i, 2, 0), block(i, 2, 0), device(0, 1), 7)
        push(i, 11, block(i, 2, 0), block(i, 2, 0), device(0, -1), 11)
        hand_over(i, 2, 0)

    def g4(i):
        take(i, 5, block(i, -1, -1))
        push(i, 13, block(i, -1, -1), block(i, -1, -1), device(0, 1), 13)
        hand_over(i, -1, -1)
        take(i, 9, block(i, -1, 1))
        hand_over(i, -1, 1)
        take(i, 10, block(i, 1, 1))
        push(i, 14, block(i, 1, 1), block(i, 1, 1), device(0, -1), 14)
        hand_over(i, 1, 1)
        take(i, 6, block(i, 1, -1))
        hand_over(i, 1, -1)

    def g5(i):
        take(i, 11, block(i, 2, 1))
        push(i, 15, block(i, 2, 1), block(i, 2, 1), device(0, -1), 15)
        hand_over(i, 2, 1)
        take(i, 7, block(i, 2, -1))
        hand_over(i, 2, -1)
        take(i, 12, block(i, 0, 2))
        hand_over(i, 0, 2)

    def g6(i):
        for slot, da in ((13, -1), (14, 1), (15, 2)):
            take(i, slot, block(i, da, 2))
            hand_over(i, da, 2)

    def ready(i):
        full = b.full[i]
        mine, other = full.at[:, columns(i, core)], full.at[:, columns(i, 1 - core)]
        remote(mine, other, b.near_send.at[i], b.near_recv.at[i], sibling).wait()
        pltpu.make_async_copy(b.unit[i], block(i, 0, 0), b.keep.at[i]).wait()

    def rows_of(i, where):
        return pl.ds(pl.multiple_of(where * UNIT[i], 16), UNIT[i])

    def in_line(i, a, db):
        return rows_of(i, a * stride_a + around(second, db) * stride_b)

    def back(i, slot, source, target, device_id):
        start(source, target, b.back_send.at[i, slot], b.back_recv.at[i, slot], device_id)

    def back_take(i, slot, ref):
        arrived(ref, b.back_recv.at[i, slot])

    def add_rows(i, where, extra):
        total = b.total[i]
        total[where, :] = (total[where, :].astype(F32) + extra.astype(F32)).astype(LOW)

    def add_pair(i, db):
        for a in range(4):
            where = in_line(i, a, db)
            add_rows(i, where, b.pair[i][where, :])

    def r0(i):
        start(b.away[i], b.pair[i], b.swap_send.at[i], b.swap_recv.at[i], sibling)

    def r1(i):
        total, far, near = b.total[i], b.far_b[i], b.near_b[i]
        arrived(b.pair[i], b.swap_recv.at[i])
        add_pair(i, 2)
        for n, a in enumerate((0, 1, 2, 3)):
            back(i, n, total.at[in_line(i, a, 2), :], far.at[n], device(0, 1 if a < 2 else -1))
        add_pair(i, 1)
        for a in (2, 3):
            back(i, 4 + a, total.at[in_line(i, a, 1), :], near.at[a], device(0, 1))
        add_pair(i, -1)
        for a in (0, 1):
            back(i, 8 + a, total.at[in_line(i, a, -1), :], near.at[4 + a], device(0, -1))

    def r2(i):
        total, far, near = b.total[i], b.far_b[i], b.near_b[i]
        for a in (0, 2, 1, 3):
            db, base = (1, 0) if a < 2 else (-1, 4)
            back_take(i, a, far.at[a])
            add_rows(i, in_line(i, a, db), far[a])
            back(i, 4 + base + a, total.at[in_line(i, a, db), :], near.at[base + a], device(0, db))
        add_pair(i, 0)

    def r3(i):
        half, cut = WIDTH[i] // 2, CUT[i]
        total, near, far = b.total[i], b.near_b[i], b.far_a[i]
        for n in range(8):
            back_take(i, 4 + n, near.at[n])
        for a in range(4):
            where = in_line(i, a, 0)
            value = total[where, :].astype(F32) + near[a].astype(F32) + near[4 + a].astype(F32)
            total[where, :] = value.astype(LOW)
        there = rows_of(i, chip(2, 0))
        low, high = pl.ds(0, cut), pl.ds(cut, half - cut)
        back(i, 12, total.at[there, low], far.at[:, low], device(1, 0))
        back(i, 13, total.at[there, high], far.at[:, high], device(-1, 0))

    def r4(i):
        half, cut = WIDTH[i] // 2, CUT[i]
        total, far, near = b.total[i], b.far_a[i], b.near_a[i]
        for n, cols, da in ((0, pl.ds(0, cut), 1), (1, pl.ds(cut, half - cut), -1)):
            there = rows_of(i, chip(da, 0))
            back_take(i, 12 + n, far.at[:, cols])
            value = total[there, cols].astype(F32) + far[:, cols].astype(F32)
            total[there, cols] = value.astype(LOW)
            back(i, 14 + n, total.at[there, :], near.at[n], device(da, 0))

    def tiles(group):
        n = 0
        for i in GROUPS[group]:
            for r in range(UNIT[i] // 48):
                for t in range(WIDTH[i] // 256):
                    yield n, i, slice(48 * r, 48 * r + 48), slice(128 * t, 128 * t + 128)
                    n += 1

    def share(dz):
        return pl.ds(around(depth, dz) * SHARE, SHARE)

    def z1(group):
        for i in GROUPS[group]:
            near = b.near_a[i]
            back_take(i, 14, near.at[0])
            back_take(i, 15, near.at[1])
            value = b.total[i][rows_of(i, chip(0, 0)), :].astype(F32)
            b.last[i][...] = value + near[0].astype(F32) + near[1].astype(F32)
        part = b.part.at[group]
        for n, i, r, c in tiles(group):
            part[n] = b.last[i][r, c].astype(LOW)
        for n in (1, 0, 2):
            sems = b.z_send.at[group, n], b.z_recv.at[group, n]
            start(part.at[share(n + 1)], b.parts_in.at[group, n], *sems, deep(n + 1))

    def z2(group):
        value = b.part[group, share(0)].astype(F32)
        for n in range(3):
            arrived(b.parts_in.at[group, n], b.z_recv.at[group, n])
            value = value + b.parts_in[group, n].astype(F32)
        whole = b.whole.at[group]
        whole[share(0)] = value.astype(LOW)
        for n in (1, 0, 2):
            sems = b.z_send.at[group, 3 + n], b.z_recv.at[group, 3 + n]
            start(whole.at[share(0)], whole.at[share(0)], *sems, deep(n + 1))

    finals = []

    def z3(group):
        whole = b.whole.at[group]
        for n in range(3):
            arrived(whole.at[share(-n - 1)], b.z_recv.at[group, 3 + n])
        for n, i, r, c in tiles(group):
            b.last[i][r, c] = whole[n].astype(F32)
        for i in GROUPS[group]:
            last, half = b.last[i], UNIT[i] // 2
            target = outs[i].at[:, columns(i, core)]
            copy = remote(
                last.at[pl.ds(pl.multiple_of((1 - core) * half, 8), half), :],
                target,
                b.out_send.at[i],
                b.out_recv.at[i],
                sibling,
            )
            copy.start()
            finals.append(copy)
            copy = pltpu.make_async_copy(
                last.at[pl.ds(pl.multiple_of(core * half, 8), half), :], target, b.out_local.at[i]
            )
            copy.start()
            finals.append(copy)

    rings = ((device(1, 0), device(2, 0), device(-1, 0)), (device(0, 1), device(0, 2), device(0, -1)), tuple(deep(n) for n in (1, 2, 3)))

    def small_send(step):
        source = b.small_grad if step == 0 else b.small_sum.at[step - 1]
        others = (sibling,) if step == 0 else rings[step - 1]
        base = 0 if step == 0 else 3 * step - 2
        for n, target in enumerate(others):
            start(source, b.small_in.at[base + n], b.small_send.at[base + n], b.small_recv.at[base + n], target)

    def small_take(step):
        base, count = (0, 1) if step == 0 else (3 * step - 2, 3)
        value = b.small_grad[...] if step == 0 else b.small_sum[step - 1]
        for n in range(count):
            arrived(b.small_in.at[base + n], b.small_recv.at[base + n])
            value = value + b.small_in[base + n]
        if step == 3:
            small_out[...] = value
        else:
            b.small_sum[step] = value
            small_send(step + 1)

    def lane(rows, width):
        return lax.broadcasted_iota(jnp.int32, (rows, width), 1)

    def place_vectors():
        mine = b.mine[4]
        mine[...] = jnp.zeros_like(mine)
        row, offset = 0, 0
        for size in SIZES:
            width = 32 * size
            line = jnp.concatenate([packed[0:1, :], jnp.zeros((1, width - 384), F32)], axis=1)
            line = jnp.broadcast_to(line, (8, width))
            line = pltpu.roll(line, lax.rem(index * size - offset + width, width), 1)
            at = lane(8, width)
            line = jnp.where((at >= index * size) & (at < index * size + size), line, 0.0)
            for r in range(width // WIDE):
                mine[row : row + 1, :] = line[0:1, WIDE * r : WIDE * r + WIDE]
                row += 1
            offset += size

    def prepare():
        x = tokens[...].astype(F32)
        centered = x - jnp.mean(x, axis=-1, keepdims=True)
        inverse = lax.rsqrt(jnp.mean(centered * centered, axis=-1, keepdims=True) + EPS)
        b.normal[...] = centered * inverse
        b.inverse[...] = inverse
        slot = lax.broadcasted_iota(jnp.int32, (ROWS, ROWS), 0)
        offsets = sequences[2:3, :]
        inside = (sequences[0:1, :] == index * 4 + depth) & (slot >= offsets) & (slot < offsets + sequences[1:2, :])
        ones = jnp.where(inside, 1.0, 0.0)
        valid = jnp.sum(ones, axis=1, keepdims=True)
        b.valid[...] = valid
        position = jnp.sum(jnp.where(inside, (slot - offsets).astype(F32), 0.0), axis=1, keepdims=True)
        rest = jnp.where(lane(ROWS, 128) == 0, 1.0 - valid, 0.0)
        member = jnp.concatenate([ones, rest], axis=1).astype(LOW)
        same = mm_nt(member, member)
        b.bias[...] = jnp.where((same > 0.5) & (lane(ROWS, ROWS) <= slot), 0.0, -1e30)
        at = lane(1, 128)
        freq = jnp.zeros((1, 128), F32)
        for n in range(ROT // 2):
            freq = jnp.where((at & 7) == n, 10000.0 ** (-2.0 * n / ROT), freq)
        angle = position * freq
        within = lane(ROWS, 128) & (HD - 1)
        sine = jnp.sin(angle)
        turn = b.turn
        turn[0] = jnp.where(within < ROT, jnp.cos(angle), 1.0)
        turn[1] = jnp.where(within < ROT // 2, -sine, 0.0)
        turn[2] = jnp.where((within >= ROT // 2) & (within < ROT), sine, 0.0)
        upstream = cotangent[...].astype(F32) * valid
        b.upstream[...] = upstream.astype(LOW)
        grads = b.small_grad
        grads[...] = jnp.zeros_like(grads)
        grads[7:8, :] = jnp.sum(upstream, axis=0, keepdims=True)

    def rotate(value, sign):
        turn = b.turn
        moved = pltpu.roll(value, 120, 1) * turn[1] + pltpu.roll(value, 8, 1) * turn[2]
        return value * turn[0] + moved if sign > 0 else value * turn[0] - moved

    def vector(row, low=0, size=WIDE):
        return b.vectors[row : row + 1, low : low + size]

    def norms():
        values = jnp.sum(b.full[4][...].astype(F32).reshape(16, 16, WIDE), axis=0)
        b.vectors[...] = values
        normal = b.normal[...]
        one = (normal * vector(9) + vector(10)).astype(LOW)
        b.xn1[...] = one
        b.xt[...] = one.T
        b.xn2[...] = (normal * vector(11) + vector(12)).astype(LOW)

    def project(t):
        value = mm(b.xn1[...], b.full[0][:, 256 * t : 256 * t + 256]) + vector(t // 3, 256 * (t % 3), 256)
        for n in range(2):
            part = value[:, 128 * n : 128 * n + 128]
            if t < 6:
                part = rotate(part, 1).astype(LOW)
            if t < 3:
                part = part.astype(F32) * HD ** (-0.5)
            b.qkv[:, 256 * t + 128 * n : 256 * t + 128 * n + 128] = part.astype(LOW)

    def context_back():
        b.dcontext[...] = mm_nt(b.upstream[...], b.full[1][...]).astype(LOW)

    def heads(p):
        cols = slice(128 * p, 128 * p + 128)
        q = b.qkv[:, 128 * p : 128 * p + 128]
        k = b.qkv[:, WIDE + 128 * p : WIDE + 128 * p + 128]
        v = b.qkv[:, 2 * WIDE + 128 * p : 2 * WIDE + 128 * p + 128]
        dc = b.dcontext[:, cols]
        lower = lane(ROWS, 128) < HD
        results = []
        for h in range(2):
            mask = jnp.where(lower if h == 0 else ~lower, 1.0, 0.0).astype(LOW)
            scores = mm_nt(q * mask, k) + b.bias[...]
            e = jnp.exp(scores - jnp.max(scores, axis=-1, keepdims=True))
            soft = e * (1.0 / jnp.sum(e, axis=-1, keepdims=True))
            probs = soft.astype(LOW)
            dprobs = mm_nt(dc * mask, v)
            ds = (soft * (dprobs - jnp.sum(soft * dprobs, axis=-1, keepdims=True))).astype(LOW)
            results.append((mm(probs, v), mm_tn(probs, dc), mm(ds, k), mm_tn(ds, q)))
        context, dv, dq, dk = (jnp.where(lower, one, two) for one, two in zip(*results))
        b.context[:, cols] = context.astype(LOW)
        dq = rotate(dq * HD ** (-0.5), -1).astype(LOW)
        dk = rotate(dk, -1).astype(LOW)
        dv = dv.astype(LOW)
        for n, value in enumerate((dq, dk, dv)):
            b.dqkv[:, WIDE * n + 128 * p : WIDE * n + 128 * p + 128] = value
            total = jnp.sum(value.astype(F32), axis=0, keepdims=True)
            b.small_grad[n : n + 1, cols] = total

    def grad_out():
        turned = b.context[...].T
        b.away[1][...] = mm(turned, b.upstream[:, columns(OUT, 1 - core)]).astype(LOW)
        b.total[1][...] = mm(turned, b.upstream[:, columns(OUT, core)]).astype(LOW)

    def grad_wide(i, source, which, target):
        step = 384
        for t in range(WIDTH[i] // 2 // step):
            at = pl.multiple_of(which * (WIDTH[i] // 2) + step * t, 128)
            target[:, step * t : step * t + step] = mm(b.xt[...], source[:, pl.ds(at, step)]).astype(LOW)

    def hidden(t):
        cols = slice(512 * t, 512 * t + 512)
        h = mm(b.xn2[...], b.full[2][:, cols])
        at = 512 * t
        pieces = []
        for n in range(2):
            pieces.append(vector(3 + (at + 256 * n) // WIDE, (at + 256 * n) % WIDE, 256))
        h = h + jnp.concatenate(pieces, axis=1)
        cdf = 0.5 * (1.0 + lax.erf(h * INV_ROOT_TWO))
        b.act[:, cols] = (h * cdf).astype(LOW)
        b.slope[:, cols] = cdf + h * jnp.exp(-0.5 * h * h) * INV_ROOT_TWO_PI

    def grad_down(t):
        rows = slice(512 * t, 512 * t + 512)
        turned = b.act[:, rows].T
        b.away[3][rows, :] = mm(turned, b.upstream[:, columns(DOWN, 1 - core)]).astype(LOW)
        b.total[3][rows, :] = mm(turned, b.upstream[:, columns(DOWN, core)]).astype(LOW)

    def hidden_back(t):
        cols = slice(512 * t, 512 * t + 512)
        value = (mm_nt(b.upstream[...], b.full[3][cols, :]) * b.slope[:, cols]).astype(LOW)
        b.dh[:, cols] = value
        total = jnp.sum(value.astype(F32), axis=0, keepdims=True)
        for n in range(2):
            at = 512 * t + 256 * n
            row, low = 3 + at // WIDE, at % WIDE
            b.small_grad[row : row + 1, low : low + 256] = total[:, 256 * n : 256 * n + 256]

    def turn_xn2():
        b.xt[...] = b.xn2[...].T

    def finish_forward():
        value = mm(b.context[...], b.full[1][...]) + mm(b.act[...], b.full[3][...])
        value = value + (vector(7) + vector(8)) + tokens[...].astype(F32)
        mixed[...] = (value * b.valid[...]).astype(LOW)

    def norm_back(upstream, gain, row):
        normal = b.normal[...]
        b.small_grad[row : row + 1, :] = jnp.sum(upstream * normal, axis=0, keepdims=True)
        b.small_grad[row + 1 : row + 2, :] = jnp.sum(upstream, axis=0, keepdims=True)
        scaled = upstream * gain
        centre = jnp.mean(scaled, axis=-1, keepdims=True)
        slope = jnp.mean(scaled * normal, axis=-1, keepdims=True)
        return b.inverse[...] * (scaled - centre - normal * slope)

    def back_one():
        grad = mm_nt(b.dqkv[...], b.full[0][...])
        b.dx[...] = b.upstream[...].astype(F32) + norm_back(grad, vector(9), 8)

    def back_two():
        grad = mm_nt(b.dh[...], b.full[2][...])
        grad_tokens[...] = (b.dx[...] + norm_back(grad, vector(11), 10)).astype(LOW)

    for i in range(GRADS):
        b.mine[i][...] = own[i][...].astype(F32)
    place_vectors()
    targets = [device(1, 0), device(-1, 0), device(2, 0), device(0, 1), device(0, -1), device(0, 2), sibling]
    targets += [deep(1), deep(2), deep(3)]
    barrier = pltpu.get_barrier_semaphore()
    for target in targets:
        pl.semaphore_signal(barrier, inc=1, device_id=target, device_id_type=MESH)
    pl.semaphore_wait(barrier, len(targets))

    attention = (SMALL, QKV, OUT)
    for i in (SMALL, QKV, OUT, UP, DOWN):
        swap_own(i)
    for i in (SMALL, QKV, OUT, UP, DOWN):
        g1(i)
    prepare()
    for step in (g2, g3):
        for i in (SMALL, QKV, OUT, UP, DOWN):
            step(i)
    for step in (g4, g5, g6):
        for i in attention:
            step(i)
        if step is not g6:
            step(UP)
            step(DOWN)
    ready(SMALL)
    norms()
    ready(QKV)
    for t in range(9):
        project(t)
    ready(OUT)
    context_back()
    g6(UP)
    heads(0)
    g6(DOWN)
    for p in range(1, 6):
        heads(p)
    grad_out()
    r0(OUT)
    grad_wide(QKV, b.dqkv, 1 - core, b.away[0])
    r0(QKV)
    r1(OUT)
    grad_wide(QKV, b.dqkv, core, b.total[0])
    r1(QKV)
    ready(UP)
    for t in range(6):
        hidden(t)
        if t == 2:
            r2(OUT)
    for t in range(6):
        grad_down(t)
    r0(DOWN)
    r2(QKV)
    turn_xn2()
    ready(DOWN)
    r1(DOWN)
    for t in range(6):
        hidden_back(t)
    grad_wide(UP, b.dh, 1 - core, b.away[2])
    r0(UP)
    grad_wide(UP, b.dh, core, b.total[2])
    r1(UP)
    r3(OUT)
    r3(QKV)
    r2(DOWN)
    back_one()
    r2(UP)
    r4(OUT)
    r4(QKV)
    back_two()
    small_send(0)
    r3(DOWN)
    z1(0)
    small_take(0)
    r3(UP)
    r4(DOWN)
    finish_forward()
    small_take(1)
    z2(0)
    r4(UP)
    z1(1)
    small_take(2)
    z1(2)
    z3(0)
    z2(1)
    z2(2)
    small_take(3)
    z3(1)
    z3(2)
    for copy in finals:
        copy.wait()
    for copy in started:
        copy.wait_send()


VECTORS = ((0, 72), (7, 24), (3, 96), (7, 24), (8, 24), (9, 24), (10, 24), (11, 24))


def deliver(*refs):
    count = 2 + GRADS
    sums = refs[count]
    ends = refs[count + 1 : 2 * count + 1]
    parts = refs[2 * count + 1 :]
    for n in range(count):
        ends[n][...] = refs[n][...]
    index = lax.axis_index("shard")
    for (row, size), part in zip(VECTORS, parts):
        width = 32 * size
        line = jnp.concatenate([sums[row + r : row + r + 1, :] for r in range(width // WIDE)], axis=1)
        line = pltpu.roll(jnp.broadcast_to(line, (8, width)), lax.rem(width - index * size, width), 1)
        part[...] = line[0:1, :size]


def per_device(
    tokens,
    cotangent,
    w_qkv,
    b_qkv,
    w_out,
    b_out,
    w_up,
    b_up,
    w_down,
    b_down,
    ln1_gain,
    ln1_bias,
    ln2_gain,
    ln2_bias,
    seq_device,
    seq_lengths,
    seq_offsets,
):
    index = lax.axis_index("shard")
    packed = jnp.concatenate(
        [b_qkv, b_up, b_out, b_down, ln1_gain, ln1_bias, ln2_gain, ln2_bias, jnp.zeros((72,), LOW)]
    ).astype(F32)
    packed = jnp.broadcast_to(packed[None, :], (8, 384))
    sequences = jnp.stack([seq_device, seq_lengths, seq_offsets] + [seq_device] * 5)
    vmem = pl.BlockSpec(memory_space=pltpu.VMEM)
    anywhere = pl.BlockSpec(memory_space=pl.ANY)
    rows = jax.ShapeDtypeStruct((ROWS, WIDE), LOW)
    shapes = [rows, rows] + [jax.ShapeDtypeStruct((UNIT[i] // 2, WIDTH[i]), F32) for i in range(GRADS)]
    results = pl.pallas_call(
        kernel,
        out_shape=shapes + [jax.ShapeDtypeStruct((16, WIDE), F32)],
        in_specs=[vmem] * 8,
        out_specs=[vmem] * 2 + [anywhere] * GRADS + [vmem],
        scratch_shapes=KINDS,
        compiler_params=pltpu.CompilerParams(
            collective_id=0, has_side_effects=True, vmem_limit_bytes=63 * 1024 * 1024
        ),
    )(tokens, cotangent, packed, sequences, w_qkv, w_out, w_up, w_down)
    results = pl.pallas_call(
        deliver,
        out_shape=shapes + [jax.ShapeDtypeStruct((1, size), F32) for _, size in VECTORS],
        in_specs=[vmem] * 7,
        out_specs=[vmem] * (6 + len(VECTORS)),
    )(*results)
    mixed, grad_tokens, out_qkv, out_out, out_up, out_down = results[:6]
    b_qkv, b_out, b_up, b_down, gain1, bias1, gain2, bias2 = (value.reshape(-1) for value in results[6:])
    return (
        mixed,
        grad_tokens,
        out_qkv,
        b_qkv,
        out_out,
        b_out,
        out_up,
        b_up,
        out_down,
        b_down,
        gain1,
        bias1,
        gain2,
        bias2,
    )


def solution(mesh):
    return jax.shard_map(
        per_device,
        mesh=mesh,
        in_specs=(
            P(("shard", "replica"), None),
            P(("shard", "replica"), None),
            P("shard", None),
            P("shard"),
            P("shard", None),
            P("shard"),
            P("shard", None),
            P("shard"),
            P("shard", None),
            P("shard"),
            P("shard"),
            P("shard"),
            P("shard"),
            P("shard"),
            P(),
            P(),
            P(),
        ),
        out_specs=(
            P(("shard", "replica"), None),
            P(("shard", "replica"), None),
            P("shard", None),
            P("shard"),
            P("shard", None),
            P("shard"),
            P("shard", None),
            P("shard"),
            P("shard", None),
            P("shard"),
            P("shard"),
            P("shard"),
            P("shard"),
            P("shard"),
        ),
        check_vma=False,
    )
```

```python
import types

import jax
import jax.numpy as jnp
from jax import lax
from jax.experimental import pallas as pl
from jax.experimental.pallas import tpu as pltpu
from jax.sharding import PartitionSpec as P

HD = 64
ROT = 16
WIDE = 768
ROWS = 256
EPS = 1e-05
INV_ROOT_TWO = 0.7071067811865476
INV_ROOT_TWO_PI = 0.3989422804014327
MESH = pl.DeviceIdType.MESH
F32 = jnp.float32
LOW = jnp.bfloat16

UNIT = (48, 48, 48, 192, 16)
WIDTH = (2304, 768, 3072, 768, 768)
CUT = (640, 256, 768, 128, 256)
QKV, OUT, UP, DOWN, SMALL = range(5)
PARTS = 5
GRADS = 4
GROUPS = ((OUT, QKV), (UP,))
SHARE = 3


def mm(a, b):
    return jnp.dot(a, b, preferred_element_type=F32)


def mm_nt(a, b):
    return lax.dot_general(a, b, (((1,), (1,)), ((), ())), preferred_element_type=F32)


def mm_tn(a, b):
    return lax.dot_general(a, b, (((0,), (0,)), ((), ())), preferred_element_type=F32)


def around(value, shift):
    return lax.rem(value + shift + 4, 4)


def remote(source, target, sent, received, device):
    return pltpu.make_async_remote_copy(
        src_ref=source, dst_ref=target, send_sem=sent, recv_sem=received, device_id=device, device_id_type=MESH
    )


def scratch():
    dma = pltpu.SemaphoreType.DMA
    half = [width // 2 for width in WIDTH]
    own = [UNIT[i] // 2 for i in range(GRADS)] + [16]

    def each(count, shape, dtype=LOW):
        return [pltpu.VMEM(shape(i), dtype) for i in range(count)]

    groups = len(GROUPS)
    return dict(
        mine=each(PARTS, lambda i: (own[i], WIDTH[i]), F32),
        his=each(PARTS, lambda i: (own[i], half[i]), F32),
        unit=each(PARTS, lambda i: (UNIT[i], half[i])),
        full=each(PARTS, lambda i: (16 * UNIT[i], WIDTH[i])),
        total=each(GRADS, lambda i: (16, 4, 48, half[i]) if i == DOWN else (16 * UNIT[i], half[i])),
        away=each(GRADS, lambda i: (16, 4, 48, half[i]) if i == DOWN else (16 * UNIT[i], half[i])),
        pair=each(GRADS, lambda i: (16, 4, 48, half[i]) if i == DOWN else (16 * UNIT[i], half[i])),
        far_b=each(DOWN, lambda i: (4, 48, half[i])),
        near_b=each(GRADS, lambda i: (12 if i == DOWN else 8, 48, half[i])),
        near_a=each(GRADS, lambda i: (3, 48, half[i])),
        deep_far=pltpu.VMEM((2, 8, 48, 384), LOW),
        deep_near=pltpu.VMEM((2, 16, 48, 384), LOW),
        deep_last=pltpu.VMEM((4, 48, 384), LOW),
        down_send=dma((9,)),
        down_recv=dma((9,)),
        last=each(GRADS, lambda i: (UNIT[i], half[i]), F32),
        part=pltpu.VMEM((groups, 4 * SHARE, 48, 128), LOW),
        parts_in=pltpu.VMEM((groups, 3, SHARE, 48, 128), LOW),
        whole=pltpu.VMEM((groups, 4 * SHARE, 48, 128), LOW),
        small_grad=pltpu.VMEM((16, WIDE), F32),
        small_in=pltpu.VMEM((10, 16, WIDE), F32),
        small_sum=pltpu.VMEM((3, 16, WIDE), F32),
        vectors=pltpu.VMEM((16, WIDE), F32),
        normal=pltpu.VMEM((ROWS, WIDE), F32),
        inverse=pltpu.VMEM((ROWS, 1), F32),
        valid=pltpu.VMEM((ROWS, 1), F32),
        bias=pltpu.VMEM((ROWS, ROWS), F32),
        turn=pltpu.VMEM((3, ROWS, 128), F32),
        upstream=pltpu.VMEM((ROWS, WIDE), LOW),
        xn1=pltpu.VMEM((ROWS, WIDE), LOW),
        xn2=pltpu.VMEM((ROWS, WIDE), LOW),
        xt=pltpu.VMEM((WIDE, ROWS), LOW),
        qkv=pltpu.VMEM((ROWS, 3 * WIDE), LOW),
        dcontext=pltpu.VMEM((ROWS, WIDE), LOW),
        context=pltpu.VMEM((ROWS, WIDE), LOW),
        dqkv=pltpu.VMEM((ROWS, 3 * WIDE), LOW),
        act=pltpu.VMEM((ROWS, 4 * WIDE), LOW),
        slope=pltpu.VMEM((ROWS, 4 * WIDE), F32),
        dh=pltpu.VMEM((ROWS, 4 * WIDE), LOW),
        dx=pltpu.VMEM((ROWS, WIDE), F32),
        pair_send=dma((PARTS,)),
        pair_recv=dma((PARTS,)),
        send=dma((PARTS, 16)),
        recv=dma((PARTS, 16)),
        near_send=dma((PARTS,)),
        near_recv=dma((PARTS,)),
        keep=dma((PARTS,)),
        swap_send=dma((GRADS,)),
        swap_recv=dma((GRADS,)),
        back_send=dma((GRADS, 16)),
        back_recv=dma((GRADS, 16)),
        z_send=dma((groups, 6)),
        z_recv=dma((groups, 6)),
        small_send=dma((10,)),
        small_recv=dma((10,)),
        out_send=dma((GRADS,)),
        out_recv=dma((GRADS,)),
        out_local=dma((GRADS,)),
    )


KINDS, TREE = jax.tree.flatten(scratch())
SIZES = (72, 96, 24, 24, 24, 24, 24, 24)


def kernel(*refs):
    tokens, cotangent, packed, sequences = refs[:4]
    own = refs[4:8]
    mixed, grad_tokens = refs[8:10]
    outs = refs[10:14]
    small_out = refs[14]
    b = types.SimpleNamespace(**jax.tree.unflatten(TREE, refs[15:]))

    index = lax.axis_index("shard")
    depth = lax.axis_index("replica")
    core = lax.rem(index, 2)
    place = index // 2
    across, along = lax.rem(place, 4), place // 4
    first = across * (1 - core) + along * core
    second = along * (1 - core) + across * core
    stride_a, stride_b = 1 + 3 * core, 4 - 3 * core

    def chip(da, db):
        return around(first, da) * stride_a + around(second, db) * stride_b

    def device(da, db):
        return {"shard": chip(da, db) * 2 + core}

    def deep(dz):
        return {"replica": around(depth, dz)}

    sibling = {"shard": place * 2 + 1 - core}
    started = []

    def start(source, target, sent, received, device_id):
        copy = remote(source, target, sent, received, device_id)
        copy.start()
        started.append(copy)

    def arrived(ref, received):
        remote(ref, ref, b.send.at[0, 0], received, sibling).wait_recv()

    def columns(i, which):
        half = WIDTH[i] // 2
        return pl.ds(pl.multiple_of(which * half, 128), half)

    def block(i, da, db, low=0, high=None):
        u, half = UNIT[i], WIDTH[i] // 2
        high = half if high is None else high
        return b.full[i].at[
            pl.ds(pl.multiple_of(chip(da, db) * u, 16), u),
            pl.ds(pl.multiple_of(core * half + low, 128), high - low),
        ]

    def push(i, slot, source, target, device_id, arrival):
        start(source, target, b.send.at[i, slot], b.recv.at[i, arrival], device_id)

    def hand_over(i, da, db, source=None):
        target = block(i, da, db)
        source = target if source is None else source
        remote(source, target, b.near_send.at[i], b.near_recv.at[i], sibling).start()

    def take(i, slot, ref):
        arrived(ref, b.recv.at[i, slot])

    def swap_own(i):
        start(b.mine[i].at[:, columns(i, 1 - core)], b.his[i], b.pair_send.at[i], b.pair_recv.at[i], sibling)

    def g1(i):
        mine_ref, unit = b.mine[i], b.unit[i]
        arrived(b.his[i], b.pair_recv.at[i])
        half = WIDTH[i] // 2
        mine = jnp.where(core == 0, mine_ref[:, :half], mine_ref[:, half:])
        other = b.his[i][...]
        if i == SMALL:
            unit[...] = (mine + other).astype(LOW)
        else:
            rows = [jnp.where(core == 0, mine, other), jnp.where(core == 0, other, mine)]
            unit[...] = jnp.concatenate(rows, axis=0).astype(LOW)
        here = block(i, 0, 0)
        push(i, 0, unit, here, device(1, 0), 0)
        push(i, 1, unit, here, device(-1, 0), 1)
        push(i, 2, unit, here, device(0, 1), 4)
        push(i, 3, unit, here, device(0, -1), 8)
        hand_over(i, 0, 0, unit)
        pltpu.make_async_copy(unit, here, b.keep.at[i]).start()

    def g2(i):
        half, cut = WIDTH[i] // 2, CUT[i]
        take(i, 0, block(i, -1, 0))
        push(i, 4, block(i, -1, 0, 0, cut), block(i, -1, 0, 0, cut), device(1, 0), 2)
        push(i, 5, block(i, -1, 0), block(i, -1, 0), device(0, 1), 5)
        push(i, 6, block(i, -1, 0), block(i, -1, 0), device(0, -1), 9)
        hand_over(i, -1, 0)
        take(i, 1, block(i, 1, 0))
        push(i, 7, block(i, 1, 0, cut, half), block(i, 1, 0, cut, half), device(-1, 0), 3)
        push(i, 8, block(i, 1, 0), block(i, 1, 0), device(0, 1), 6)
        push(i, 9, block(i, 1, 0), block(i, 1, 0), device(0, -1), 10)
        hand_over(i, 1, 0)

    def g3(i):
        half, cut = WIDTH[i] // 2, CUT[i]
        take(i, 4, block(i, 0, -1))
        push(i, 12, block(i, 0, -1), block(i, 0, -1), device(0, 1), 12)
        hand_over(i, 0, -1)
        take(i, 8, block(i, 0, 1))
        hand_over(i, 0, 1)
        take(i, 2, block(i, 2, 0, 0, cut))
        take(i, 3, block(i, 2, 0, cut, half))
        push(i, 10, block(i, 2, 0), block(i, 2, 0), device(0, 1), 7)
        push(i, 11, block(i, 2, 0), block(i, 2, 0), device(0, -1), 11)
        hand_over(i, 2, 0)

    def g4(i):
        take(i, 5, block(i, -1, -1))
        push(i, 13, block(i, -1, -1), block(i, -1, -1), device(0, 1), 13)
        hand_over(i, -1, -1)
        take(i, 9, block(i, -1, 1))
        hand_over(i, -1, 1)
        take(i, 10, block(i, 1, 1))
        push(i, 14, block(i, 1, 1), block(i, 1, 1), device(0, -1), 14)
        hand_over(i, 1, 1)
        take(i, 6, block(i, 1, -1))
        hand_over(i, 1, -1)

    def g5(i):
        take(i, 11, block(i, 2, 1))
        push(i, 15, block(i, 2, 1), block(i, 2, 1), device(0, -1), 15)
        hand_over(i, 2, 1)
        take(i, 7, block(i, 2, -1))
        hand_over(i, 2, -1)
        take(i, 12, block(i, 0, 2))
        hand_over(i, 0, 2)

    def g6(i):
        for slot, da in ((13, -1), (14, 1), (15, 2)):
            take(i, slot, block(i, da, 2))
            hand_over(i, da, 2)

    def ready(i):
        full = b.full[i]
        mine, other = full.at[:, columns(i, core)], full.at[:, columns(i, 1 - core)]
        remote(mine, other, b.near_send.at[i], b.near_recv.at[i], sibling).wait()
        pltpu.make_async_copy(b.unit[i], block(i, 0, 0), b.keep.at[i]).wait()

    def rows_of(i, where):
        return pl.ds(pl.multiple_of(where * UNIT[i], 16), UNIT[i])

    def in_line(a, db):
        return a * stride_a + around(second, db) * stride_b

    def cell(i, where, cols=slice(None)):
        if i == DOWN:
            return b.total[i].at[where, depth, :, cols]
        return b.total[i].at[rows_of(i, where), cols]

    def back(i, slot, source, target, device_id):
        start(source, target, b.back_send.at[i, slot], b.back_recv.at[i, slot], device_id)

    def back_take(i, slot, ref):
        arrived(ref, b.back_recv.at[i, slot])

    def add_pair(i, db):
        for a in range(4):
            where = rows_of(i, in_line(a, db))
            b.total[i][where, :] = b.total[i][where, :] + b.pair[i][where, :]

    def r0(i):
        start(b.away[i], b.pair[i], b.swap_send.at[i], b.swap_recv.at[i], sibling)

    def r1(i):
        near = b.near_b[i]
        if i == DOWN:
            for n, db in enumerate((2, 1, -1)):
                for a in range(4):
                    back(i, 4 * n + a, cell(i, in_line(a, db)), near.at[4 * n + a], device(0, db))
            return
        arrived(b.pair[i], b.swap_recv.at[i])
        add_pair(i, 2)
        for a in range(4):
            back(i, a, cell(i, in_line(a, 2)), b.far_b[i].at[a], device(0, 1 if a < 2 else -1))
        add_pair(i, 1)
        for a in (2, 3):
            back(i, 4 + a, cell(i, in_line(a, 1)), near.at[a], device(0, 1))
        add_pair(i, -1)
        for a in (0, 1):
            back(i, 8 + a, cell(i, in_line(a, -1)), near.at[4 + a], device(0, -1))

    def r2(i):
        far, near = b.far_b[i], b.near_b[i]
        for a in (0, 2, 1, 3):
            db, base = (1, 0) if a < 2 else (-1, 4)
            here = cell(i, in_line(a, db))
            back_take(i, a, far.at[a])
            here[...] = here[...] + far[a]
            back(i, 4 + base + a, here, near.at[base + a], device(0, db))
        add_pair(i, 0)

    def r3(i):
        near = b.near_b[i]
        first_slot, lines = (0, 3) if i == DOWN else (4, 2)
        for n in range(4 * lines):
            back_take(i, first_slot + n, near.at[n])
        for a in range(4):
            here = cell(i, in_line(a, 0))
            value = here[...].astype(F32)
            for n in range(lines):
                value = value + near[4 * n + a].astype(F32)
            here[...] = value.astype(LOW)
        for n, da in enumerate((2, 1, -1)):
            back(i, 12 + n, cell(i, chip(da, 0)), b.near_a[i].at[n], device(da, 0))

    def r5(i):
        near = b.near_a[i]
        value = cell(i, chip(0, 0))[...].astype(F32)
        for n in range(3):
            back_take(i, 12 + n, near.at[n])
            value = value + near[n].astype(F32)
        return value

    def pieces(part, dz):
        return b.total[DOWN].at[8 * part : 8 * part + 8, around(depth, dz)]

    def down(slot, source, target, dz):
        start(source, target, b.down_send.at[slot], b.down_recv.at[slot], deep(dz))

    def e1():
        arrived(b.pair[DOWN], b.swap_recv.at[DOWN])
        near = b.deep_near
        for dz in (2, 1, -1, 0):
            at = around(depth, dz)
            b.total[DOWN][:, at] = b.total[DOWN][:, at] + b.pair[DOWN][:, at]
            if dz == 2:
                down(0, pieces(0, 2), b.deep_far.at[0], 1)
                down(1, pieces(1, 2), b.deep_far.at[1], -1)
            elif dz == 1:
                down(2, pieces(1, 1), near.at[0, 8:16], 1)
            elif dz == -1:
                down(3, pieces(0, -1), near.at[1, 0:8], -1)

    def e2():
        for part, dz in ((0, 1), (1, -1)):
            here = pieces(part, dz)
            arrived(b.deep_far.at[part], b.down_recv.at[part])
            here[...] = here[...] + b.deep_far[part]
            down(4 + part, here, b.deep_near.at[part, 8 * part : 8 * part + 8], dz)

    def e3():
        near = b.deep_near
        for part in range(2):
            arrived(near.at[0, 8 * part : 8 * part + 8], b.down_recv.at[4 if part == 0 else 2])
            arrived(near.at[1, 8 * part : 8 * part + 8], b.down_recv.at[3 if part == 0 else 5])
            here = pieces(part, 0)
            value = here[...].astype(F32)
            for n in range(2):
                value = value + near[n, 8 * part : 8 * part + 8].astype(F32)
            here[...] = value.astype(LOW)

    def e4():
        last = b.deep_last
        last[depth] = r5(DOWN).astype(LOW)
        for n in (1, 0, 2):
            down(6 + n, last.at[depth], last.at[depth], n + 1)

    def e5():
        last = b.deep_last
        for n in range(3):
            arrived(last.at[around(depth, -n - 1)], b.down_recv.at[6 + n])
        for n in range(4):
            b.last[DOWN][48 * n : 48 * n + 48, :] = last[n].astype(F32)
        hand_out(DOWN)

    def tiles(group):
        n = 0
        for i in GROUPS[group]:
            for r in range(UNIT[i] // 48):
                for t in range(WIDTH[i] // 256):
                    yield n, i, slice(48 * r, 48 * r + 48), slice(128 * t, 128 * t + 128)
                    n += 1

    def share(dz):
        return pl.ds(around(depth, dz) * SHARE, SHARE)

    def z1(group):
        for i in GROUPS[group]:
            b.last[i][...] = r5(i)
        part = b.part.at[group]
        for n, i, r, c in tiles(group):
            part[n] = b.last[i][r, c].astype(LOW)
        for n in (1, 0, 2):
            sems = b.z_send.at[group, n], b.z_recv.at[group, n]
            start(part.at[share(n + 1)], b.parts_in.at[group, n], *sems, deep(n + 1))

    def z2(group):
        value = b.part[group, share(0)].astype(F32)
        for n in range(3):
            arrived(b.parts_in.at[group, n], b.z_recv.at[group, n])
            value = value + b.parts_in[group, n].astype(F32)
        whole = b.whole.at[group]
        whole[share(0)] = value.astype(LOW)
        for n in (1, 0, 2):
            sems = b.z_send.at[group, 3 + n], b.z_recv.at[group, 3 + n]
            start(whole.at[share(0)], whole.at[share(0)], *sems, deep(n + 1))

    finals = []

    def z3(group):
        whole = b.whole.at[group]
        for n in range(3):
            arrived(whole.at[share(-n - 1)], b.z_recv.at[group, 3 + n])
        for n, i, r, c in tiles(group):
            b.last[i][r, c] = whole[n].astype(F32)
        for i in GROUPS[group]:
            hand_out(i)

    def hand_out(i):
        last, half = b.last[i], UNIT[i] // 2
        target = outs[i].at[:, columns(i, core)]
        copy = remote(
            last.at[pl.ds(pl.multiple_of((1 - core) * half, 8), half), :], target, b.out_send.at[i], b.out_recv.at[i], sibling
        )
        copy.start()
        finals.append(copy)
        source = last.at[pl.ds(pl.multiple_of(core * half, 8), half), :]
        copy = pltpu.make_async_copy(source, target, b.out_local.at[i])
        copy.start()
        finals.append(copy)

    rings = ((device(1, 0), device(2, 0), device(-1, 0)), (device(0, 1), device(0, 2), device(0, -1)), tuple(deep(n) for n in (1, 2, 3)))

    def small_send(step):
        source = b.small_grad if step == 0 else b.small_sum.at[step - 1]
        others = (sibling,) if step == 0 else rings[step - 1]
        base = 0 if step == 0 else 3 * step - 2
        for n, target in enumerate(others):
            start(source, b.small_in.at[base + n], b.small_send.at[base + n], b.small_recv.at[base + n], target)

    def small_take(step):
        base, count = (0, 1) if step == 0 else (3 * step - 2, 3)
        value = b.small_grad[...] if step == 0 else b.small_sum[step - 1]
        for n in range(count):
            arrived(b.small_in.at[base + n], b.small_recv.at[base + n])
            value = value + b.small_in[base + n]
        if step == 3:
            small_out[...] = value
        else:
            b.small_sum[step] = value
            small_send(step + 1)

    def lane(rows, width):
        return lax.broadcasted_iota(jnp.int32, (rows, width), 1)

    def place_vectors():
        mine = b.mine[4]
        mine[...] = jnp.zeros_like(mine)
        row, offset = 0, 0
        for size in SIZES:
            width = 32 * size
            line = jnp.concatenate([packed[0:1, :], jnp.zeros((1, width - 384), F32)], axis=1)
            line = jnp.broadcast_to(line, (8, width))
            line = pltpu.roll(line, lax.rem(index * size - offset + width, width), 1)
            at = lane(8, width)
            line = jnp.where((at >= index * size) & (at < index * size + size), line, 0.0)
            for r in range(width // WIDE):
                mine[row : row + 1, :] = line[0:1, WIDE * r : WIDE * r + WIDE]
                row += 1
            offset += size

    def prepare():
        x = tokens[...].astype(F32)
        centered = x - jnp.mean(x, axis=-1, keepdims=True)
        inverse = lax.rsqrt(jnp.mean(centered * centered, axis=-1, keepdims=True) + EPS)
        b.normal[...] = centered * inverse
        b.inverse[...] = inverse
        slot = lax.broadcasted_iota(jnp.int32, (ROWS, ROWS), 0)
        offsets = sequences[2:3, :]
        inside = (sequences[0:1, :] == index * 4 + depth) & (slot >= offsets) & (slot < offsets + sequences[1:2, :])
        ones = jnp.where(inside, 1.0, 0.0)
        valid = jnp.sum(ones, axis=1, keepdims=True)
        b.valid[...] = valid
        position = jnp.sum(jnp.where(inside, (slot - offsets).astype(F32), 0.0), axis=1, keepdims=True)
        rest = jnp.where(lane(ROWS, 128) == 0, 1.0 - valid, 0.0)
        member = jnp.concatenate([ones, rest], axis=1).astype(LOW)
        same = mm_nt(member, member)
        b.bias[...] = jnp.where((same > 0.5) & (lane(ROWS, ROWS) <= slot), 0.0, -1e30)
        at = lane(1, 128)
        freq = jnp.zeros((1, 128), F32)
        for n in range(ROT // 2):
            freq = jnp.where((at & 7) == n, 10000.0 ** (-2.0 * n / ROT), freq)
        angle = position * freq
        within = lane(ROWS, 128) & (HD - 1)
        sine = jnp.sin(angle)
        turn = b.turn
        turn[0] = jnp.where(within < ROT, jnp.cos(angle), 1.0)
        turn[1] = jnp.where(within < ROT // 2, -sine, 0.0)
        turn[2] = jnp.where((within >= ROT // 2) & (within < ROT), sine, 0.0)
        upstream = cotangent[...].astype(F32) * valid
        b.upstream[...] = upstream.astype(LOW)
        grads = b.small_grad
        grads[...] = jnp.zeros_like(grads)
        grads[7:8, :] = jnp.sum(upstream, axis=0, keepdims=True)

    def rotate(value, sign):
        turn = b.turn
        moved = pltpu.roll(value, 120, 1) * turn[1] + pltpu.roll(value, 8, 1) * turn[2]
        return value * turn[0] + moved if sign > 0 else value * turn[0] - moved

    def vector(row, low=0, size=WIDE):
        return b.vectors[row : row + 1, low : low + size]

    def norms():
        values = jnp.sum(b.full[4][...].astype(F32).reshape(16, 16, WIDE), axis=0)
        b.vectors[...] = values
        normal = b.normal[...]
        one = (normal * vector(9) + vector(10)).astype(LOW)
        b.xn1[...] = one
        b.xt[...] = one.T
        b.xn2[...] = (normal * vector(11) + vector(12)).astype(LOW)

    def project(t):
        value = mm(b.xn1[...], b.full[0][:, 256 * t : 256 * t + 256]) + vector(t // 3, 256 * (t % 3), 256)
        for n in range(2):
            part = value[:, 128 * n : 128 * n + 128]
            if t < 6:
                part = rotate(part, 1).astype(LOW)
            if t < 3:
                part = part.astype(F32) * HD ** (-0.5)
            b.qkv[:, 256 * t + 128 * n : 256 * t + 128 * n + 128] = part.astype(LOW)

    def context_back():
        b.dcontext[...] = mm_nt(b.upstream[...], b.full[1][...]).astype(LOW)

    def heads(p):
        cols = slice(128 * p, 128 * p + 128)
        q = b.qkv[:, 128 * p : 128 * p + 128]
        k = b.qkv[:, WIDE + 128 * p : WIDE + 128 * p + 128]
        v = b.qkv[:, 2 * WIDE + 128 * p : 2 * WIDE + 128 * p + 128]
        dc = b.dcontext[:, cols]
        lower = lane(ROWS, 128) < HD
        results = []
        for h in range(2):
            mask = jnp.where(lower if h == 0 else ~lower, 1.0, 0.0).astype(LOW)
            scores = mm_nt(q * mask, k) + b.bias[...]
            e = jnp.exp(scores - jnp.max(scores, axis=-1, keepdims=True))
            soft = e * (1.0 / jnp.sum(e, axis=-1, keepdims=True))
            probs = soft.astype(LOW)
            dprobs = mm_nt(dc * mask, v)
            ds = (soft * (dprobs - jnp.sum(soft * dprobs, axis=-1, keepdims=True))).astype(LOW)
            results.append((mm(probs, v), mm_tn(probs, dc), mm(ds, k), mm_tn(ds, q)))
        context, dv, dq, dk = (jnp.where(lower, one, two) for one, two in zip(*results))
        b.context[:, cols] = context.astype(LOW)
        dq = rotate(dq * HD ** (-0.5), -1).astype(LOW)
        dk = rotate(dk, -1).astype(LOW)
        dv = dv.astype(LOW)
        for n, value in enumerate((dq, dk, dv)):
            b.dqkv[:, WIDE * n + 128 * p : WIDE * n + 128 * p + 128] = value
            total = jnp.sum(value.astype(F32), axis=0, keepdims=True)
            b.small_grad[n : n + 1, cols] = total

    def grad_out():
        turned = b.context[...].T
        b.away[1][...] = mm(turned, b.upstream[:, columns(OUT, 1 - core)]).astype(LOW)
        b.total[1][...] = mm(turned, b.upstream[:, columns(OUT, core)]).astype(LOW)

    def grad_wide(i, source, which, target):
        step = 384
        for t in range(WIDTH[i] // 2 // step):
            at = pl.multiple_of(which * (WIDTH[i] // 2) + step * t, 128)
            target[:, step * t : step * t + step] = mm(b.xt[...], source[:, pl.ds(at, step)]).astype(LOW)

    def hidden(t):
        cols = slice(512 * t, 512 * t + 512)
        h = mm(b.xn2[...], b.full[2][:, cols])
        at = 512 * t
        pieces = []
        for n in range(2):
            pieces.append(vector(3 + (at + 256 * n) // WIDE, (at + 256 * n) % WIDE, 256))
        h = h + jnp.concatenate(pieces, axis=1)
        cdf = 0.5 * (1.0 + lax.erf(h * INV_ROOT_TWO))
        b.act[:, cols] = (h * cdf).astype(LOW)
        b.slope[:, cols] = cdf + h * jnp.exp(-0.5 * h * h) * INV_ROOT_TWO_PI

    def grad_down(t):
        turned = b.act[:, 768 * t : 768 * t + 768].T
        for target, which in ((b.away[DOWN], 1 - core), (b.total[DOWN], core)):
            value = mm(turned, b.upstream[:, columns(DOWN, which)]).astype(LOW)
            target[4 * t : 4 * t + 4] = value.reshape(4, 4, 48, 384)

    def hidden_back(t):
        cols = slice(512 * t, 512 * t + 512)
        value = (mm_nt(b.upstream[...], b.full[3][cols, :]) * b.slope[:, cols]).astype(LOW)
        b.dh[:, cols] = value
        total = jnp.sum(value.astype(F32), axis=0, keepdims=True)
        for n in range(2):
            at = 512 * t + 256 * n
            row, low = 3 + at // WIDE, at % WIDE
            b.small_grad[row : row + 1, low : low + 256] = total[:, 256 * n : 256 * n + 256]

    def turn_xn2():
        b.xt[...] = b.xn2[...].T

    def finish_forward():
        value = mm(b.context[...], b.full[1][...]) + mm(b.act[...], b.full[3][...])
        value = value + (vector(7) + vector(8)) + tokens[...].astype(F32)
        mixed[...] = (value * b.valid[...]).astype(LOW)

    def norm_back(upstream, gain, row):
        normal = b.normal[...]
        b.small_grad[row : row + 1, :] = jnp.sum(upstream * normal, axis=0, keepdims=True)
        b.small_grad[row + 1 : row + 2, :] = jnp.sum(upstream, axis=0, keepdims=True)
        scaled = upstream * gain
        centre = jnp.mean(scaled, axis=-1, keepdims=True)
        slope = jnp.mean(scaled * normal, axis=-1, keepdims=True)
        return b.inverse[...] * (scaled - centre - normal * slope)

    def back_one():
        grad = mm_nt(b.dqkv[...], b.full[0][...])
        b.dx[...] = b.upstream[...].astype(F32) + norm_back(grad, vector(9), 8)

    def back_two():
        grad = mm_nt(b.dh[...], b.full[2][...])
        grad_tokens[...] = (b.dx[...] + norm_back(grad, vector(11), 10)).astype(LOW)

    targets = [device(1, 0), device(-1, 0), device(2, 0), device(0, 1), device(0, -1), device(0, 2), sibling]
    targets += [deep(1), deep(2), deep(3)]
    barrier = pltpu.get_barrier_semaphore()
    for target in targets:
        pl.semaphore_signal(barrier, inc=1, device_id=target, device_id_type=MESH)
    for i in range(GRADS):
        b.mine[i][...] = own[i][...].astype(F32)
    pl.semaphore_wait(barrier, len(targets))
    for i in (QKV, OUT, UP, DOWN):
        swap_own(i)
    place_vectors()
    swap_own(SMALL)
    attention = (QKV, SMALL, OUT)
    for i in (QKV, SMALL, OUT, UP, DOWN):
        g1(i)
    prepare()
    for step in (g2, g3):
        for i in attention:
            step(i)
    g2(UP)
    for i in attention:
        g4(i)
    g2(DOWN)
    g3(UP)
    for i in attention:
        g5(i)
    g4(UP)
    for i in attention:
        g6(i)
    ready(SMALL)
    norms()
    ready(QKV)
    for t in range(9):
        project(t)
        if t == 1:
            g5(UP)
        if t == 4:
            g3(DOWN)
    ready(OUT)
    context_back()
    g6(UP)
    heads(0)
    g4(DOWN)
    heads(1)
    heads(2)
    g5(DOWN)
    heads(3)
    heads(4)
    heads(5)
    grad_out()
    r0(OUT)
    grad_wide(QKV, b.dqkv, 1 - core, b.away[0])
    r0(QKV)
    r1(OUT)
    grad_wide(QKV, b.dqkv, core, b.total[0])
    r1(QKV)
    ready(UP)
    hidden(0)
    hidden(1)
    g6(DOWN)
    hidden(2)
    hidden(3)
    hidden(4)
    hidden(5)
    r2(OUT)
    for t in range(4):
        grad_down(t)
    r0(DOWN)
    r2(QKV)
    e1()
    turn_xn2()
    ready(DOWN)
    for t in range(6):
        hidden_back(t)
    grad_wide(UP, b.dh, 1 - core, b.away[2])
    r0(UP)
    grad_wide(UP, b.dh, core, b.total[2])
    r1(UP)
    e2()
    r3(OUT)
    r3(QKV)
    back_one()
    r2(UP)
    back_two()
    small_send(0)
    z1(0)
    e3()
    r1(DOWN)
    small_take(0)
    r3(UP)
    z2(0)
    small_take(1)
    r3(DOWN)
    z1(1)
    finish_forward()
    small_take(2)
    e4()
    z2(1)
    z3(0)
    small_take(3)
    e5()
    z3(1)
    for copy in finals:
        copy.wait()
    for copy in started:
        copy.wait_send()


VECTORS = ((0, 72), (7, 24), (3, 96), (7, 24), (8, 24), (9, 24), (10, 24), (11, 24))


def deliver(*refs):
    count = 2 + GRADS
    sums = refs[count]
    ends = refs[count + 1 : 2 * count + 1]
    parts = refs[2 * count + 1 :]
    for n in range(count):
        ends[n][...] = refs[n][...]
    index = lax.axis_index("shard")
    for (row, size), part in zip(VECTORS, parts):
        width = 32 * size
        line = jnp.concatenate([sums[row + r : row + r + 1, :] for r in range(width // WIDE)], axis=1)
        line = pltpu.roll(jnp.broadcast_to(line, (8, width)), lax.rem(width - index * size, width), 1)
        part[...] = line[0:1, :size]


def per_device(
    tokens,
    cotangent,
    w_qkv,
    b_qkv,
    w_out,
    b_out,
    w_up,
    b_up,
    w_down,
    b_down,
    ln1_gain,
    ln1_bias,
    ln2_gain,
    ln2_bias,
    seq_device,
    seq_lengths,
    seq_offsets,
):
    index = lax.axis_index("shard")
    packed = jnp.concatenate(
        [b_qkv, b_up, b_out, b_down, ln1_gain, ln1_bias, ln2_gain, ln2_bias, jnp.zeros((72,), LOW)]
    ).astype(F32)
    packed = jnp.broadcast_to(packed[None, :], (8, 384))
    sequences = jnp.stack([seq_device, seq_lengths, seq_offsets] + [seq_device] * 5)
    vmem = pl.BlockSpec(memory_space=pltpu.VMEM)
    anywhere = pl.BlockSpec(memory_space=pl.ANY)
    rows = jax.ShapeDtypeStruct((ROWS, WIDE), LOW)
    shapes = [rows, rows] + [jax.ShapeDtypeStruct((UNIT[i] // 2, WIDTH[i]), F32) for i in range(GRADS)]
    results = pl.pallas_call(
        kernel,
        out_shape=shapes + [jax.ShapeDtypeStruct((16, WIDE), F32)],
        in_specs=[vmem] * 8,
        out_specs=[vmem] * 2 + [anywhere] * GRADS + [vmem],
        scratch_shapes=KINDS,
        compiler_params=pltpu.CompilerParams(
            collective_id=0, has_side_effects=True, vmem_limit_bytes=63 * 1024 * 1024
        ),
    )(tokens, cotangent, packed, sequences, w_qkv, w_out, w_up, w_down)
    results = pl.pallas_call(
        deliver,
        out_shape=shapes + [jax.ShapeDtypeStruct((1, size), F32) for _, size in VECTORS],
        in_specs=[vmem] * 7,
        out_specs=[vmem] * (6 + len(VECTORS)),
    )(*results)
    mixed, grad_tokens, out_qkv, out_out, out_up, out_down = results[:6]
    b_qkv, b_out, b_up, b_down, gain1, bias1, gain2, bias2 = (value.reshape(-1) for value in results[6:])
    return (
        mixed,
        grad_tokens,
        out_qkv,
        b_qkv,
        out_out,
        b_out,
        out_up,
        b_up,
        out_down,
        b_down,
        gain1,
        bias1,
        gain2,
        bias2,
    )


def solution(mesh):
    return jax.shard_map(
        per_device,
        mesh=mesh,
        in_specs=(
            P(("shard", "replica"), None),
            P(("shard", "replica"), None),
            P("shard", None),
            P("shard"),
            P("shard", None),
            P("shard"),
            P("shard", None),
            P("shard"),
            P("shard", None),
            P("shard"),
            P("shard"),
            P("shard"),
            P("shard"),
            P("shard"),
            P(),
            P(),
            P(),
        ),
        out_specs=(
            P(("shard", "replica"), None),
            P(("shard", "replica"), None),
            P("shard", None),
            P("shard"),
            P("shard", None),
            P("shard"),
            P("shard", None),
            P("shard"),
            P("shard", None),
            P("shard"),
            P("shard"),
            P("shard"),
            P("shard"),
            P("shard"),
        ),
        check_vma=False,
    )
```
